128 devices in a mesh: seq: 16 (over x, y), head: 8 (over z, core).
Axes of the slice: x: 4, y: 4, z: 4, core: 2. Of those that a mesh axis runs over, the one named last changes fastest.
Arguments:
- lin_qk: float32 [32768, 1024], P('seq', 'head'), may hold values from -6 to 6
- lin_v: float32 [32768, 4096], P('seq', 'head'), may hold values from -64 to 64
- conv_qk: float32 [3, 1024], P(None, 'head'), may hold values from -3.5 to 3.5
- conv_v: float32 [3, 4096], P(None, 'head'), may hold values from -3.5 to 3.5
- swa_qkv: float32 [32768, 3, 4096], P('seq', None, 'head'), may hold values from -5.5 to 5.5
- head_gain: float32 [4096], P('head'), may hold values from 0.5 to 13.5
Outputs:
- mixed: float32 [32768, 4096], P('seq', 'head')
The draws below stay inside these ranges and needn't reach their ends.
All inputs are finite; a program needn't handle non-finite values.
Results may differ from the reference program's by a relative error of at most 0.0003.
Values sent between devices are 32-bit elements; how exact they have to be, the bound alone decides.
A program may use at most 192 MiB of HBM per device.

```python
import math
import jax
import jax.numpy as jnp
import numpy as np
from jax import lax

H = 32
DK = 16
DV = 128
NF = 153
WIN = 64
KCONV = 3
TOK_DEV = 2048
TOKENS = 32768


def draw_lin_v(key, part):
    keys_list = jax.random.split(key, 3)
    row_scale = jnp.exp(jax.random.uniform(keys_list[0], (TOKENS, 1), jnp.float32, math.log(0.4), math.log(4.0)))
    col_scale = jnp.exp(jax.random.uniform(keys_list[1], (1, H * DV), jnp.float32, math.log(0.4), math.log(4.0)))
    entries = jnp.clip(jax.random.normal(keys_list[2], (TOKENS, H * DV), jnp.float32), -4.0, 4.0)
    return row_scale * col_scale * entries


def draw_head_gain(key, part):
    channel = jnp.arange(H * DV, dtype=jnp.int32) // DV
    ratio = channel.astype(jnp.float32) / (H - 1)
    base_gain = jax.random.uniform(key, (H * DV,), jnp.float32, 0.5, 1.5)
    return base_gain * jnp.exp(ratio * math.log(3.0))


def draw_swa_qkv(key, part):
    keys_list = jax.random.split(key, 1)
    shape_all = (TOKENS, 3, H * DV)
    return jnp.clip(jax.random.normal(keys_list[0], shape_all, jnp.float32), -4.0, 4.0)


def shard_levels(stream_key, shape, cuts, low, top_value):
    factor_of, own = 1.0, jax.random.fold_in(stream_key, 6)
    for dim, blocks in cuts:
        steps = jnp.exp(jax.random.uniform(jax.random.fold_in(own, dim), (blocks,), jnp.float32, low / len(cuts), top_value / len(cuts)))
        factor_of = factor_of * jnp.repeat(steps, shape[dim] // blocks).reshape([-1 if axis == dim else 1 for axis in range(len(shape))])
    return factor_of


def noise(stream_key, shape, width, most, pieces=(), held_as=jnp.bfloat16):
    array = jax.random.normal(stream_key, shape, jnp.float32) * width
    if len(pieces) > 0:
        array = shard_levels(stream_key, shape, pieces, -0.22, 0.18) * array
    return jnp.clip(array, min=-most, max=most).astype(held_as)


def setup_inputs(seed: int = 0) -> dict:
    splits = jax.random.split(jax.random.key(seed), 7)
    return {
        "lin_qk": noise(splits[0], (TOKENS, H * 2 * DK), 1.0, 6.0, ((0, 16), (1, 8)), jnp.float32),
        "lin_v": draw_lin_v(jax.random.fold_in(splits[6], 71), 0),
        "conv_qk": noise(splits[2], (KCONV, H * 2 * DK), KCONV ** -0.5, 3.5, ((1, 8),), jnp.float32),
        "conv_v": noise(splits[3], (KCONV, H * DV), KCONV ** -0.5, 3.5, ((1, 8),), jnp.float32),
        "swa_qkv": draw_swa_qkv(jax.random.fold_in(splits[6], 71), 0),
        "head_gain": draw_head_gain(jax.random.fold_in(splits[6], 71), 0),
    }


HIGHEST = lax.Precision.HIGHEST

def features(vectors):
    key_width = vectors.shape[-1]
    left_index, right_index = np.triu_indices(key_width)
    weights_quad = np.where(left_index == right_index, 1.0 / math.sqrt(2.0 * key_width), 1.0 / math.sqrt(key_width)).astype(np.float32)
    quadratic = vectors[..., left_index] * vectors[..., right_index] * weights_quad
    constant = jnp.ones(vectors.shape[:-1] + (1,), vectors.dtype)
    return jnp.concatenate([constant, vectors * key_width ** (-0.25), quadratic], axis=-1)

def kernel_values(query_part, key_part, pattern):
    dot_values = jnp.einsum(pattern, query_part, key_part, precision=HIGHEST)
    key_width = query_part.shape[-1]
    return 1.0 + dot_values / math.sqrt(key_width) + dot_values * dot_values / (2.0 * key_width)

def causal_conv(signal, kernel):
    length = signal.shape[0]
    padded = jnp.concatenate([jnp.zeros((kernel.shape[0] - 1, signal.shape[1]), signal.dtype), signal], axis=0)
    summed = kernel[0] * padded[0:length]
    for offset in range(1, kernel.shape[0]):
        summed = summed + kernel[offset] * padded[offset:offset + length]
    return summed

def reference(lin_qk, lin_v, conv_qk, conv_v, swa_qkv, head_gain):
    length = TOKENS
    block_rows = min(512, TOK_DEV)
    block_count = length // block_rows
    mixed_qk = causal_conv(lin_qk, conv_qk).reshape(length, H, 2 * DK)
    values = causal_conv(lin_v, conv_v).reshape(length, H, DV)
    queries = mixed_qk[..., :DK].reshape(block_count, block_rows, H, DK)
    keys_lin = mixed_qk[..., DK:].reshape(block_count, block_rows, H, DK)
    value_blocks = values.reshape(block_count, block_rows, H, DV)
    causal = jnp.tril(jnp.ones((block_rows, block_rows), bool))

    def linear_step(state, items):
        query_block, key_block, value_block = items
        kernel_vals = kernel_values(query_block, key_block, 'bhd,chd->hbc')
        kernel_vals = jnp.where(causal[None], kernel_vals, 0.0)
        local_part = jnp.einsum('hbc,chv->bhv', kernel_vals, value_block, precision=HIGHEST)
        carried = jnp.einsum('bhf,hfv->bhv', features(query_block), state, precision=HIGHEST)
        state = state + jnp.einsum('bhf,bhv->hfv', features(key_block), value_block, precision=HIGHEST)
        return (state, local_part + carried)
    initial = jnp.zeros((H, NF, DV), lin_v.dtype)
    final_state, linear_blocks = lax.scan(linear_step, initial, (queries, keys_lin, value_blocks))
    linear_mix = linear_blocks.reshape(length, H, DV)
    gain_table = head_gain.reshape(H, DV)
    linear_normed = linear_mix * lax.rsqrt(lax.optimization_barrier(jnp.mean(linear_mix * linear_mix, axis=-1, keepdims=True)) + 1e-06) * gain_table
    window_rows = min(128, TOK_DEV)
    window_count = length // window_rows
    window_queries = swa_qkv[:, 0].reshape(length, H, DV)
    zeros_rim = jnp.zeros((WIN - 1, H, DV), swa_qkv.dtype)
    padded_keys = jnp.concatenate([zeros_rim, swa_qkv[:, 1].reshape(length, H, DV)], axis=0)
    padded_values = jnp.concatenate([zeros_rim, swa_qkv[:, 2].reshape(length, H, DV)], axis=0)
    key_span = window_rows + WIN - 1
    relative = jnp.arange(key_span)[None, :] - jnp.arange(window_rows)[:, None]
    inside = (relative >= 0) & (relative <= WIN - 1)

    def window_block(block_index):
        first_row = (block_index * window_rows).astype(jnp.int32)
        query_block = lax.dynamic_slice_in_dim(window_queries, first_row, window_rows, 0)
        key_block = lax.dynamic_slice_in_dim(padded_keys, first_row, key_span, 0)
        value_block = lax.dynamic_slice_in_dim(padded_values, first_row, key_span, 0)
        scores = jnp.einsum('bhd,chd->hbc', query_block, key_block, precision=HIGHEST) / math.sqrt(DV)
        key_position = first_row + jnp.arange(key_span, dtype=jnp.int32) - (WIN - 1)
        allowed = inside & (key_position >= 0)[None, :]
        scores = jnp.where(allowed[None], scores, -1e+30)
        row_peak = lax.optimization_barrier(jnp.max(scores, axis=-1, keepdims=True))
        weights_exp = jnp.exp(scores - row_peak)
        probabilities = weights_exp / lax.optimization_barrier(jnp.sum(weights_exp, axis=-1, keepdims=True))
        return jnp.einsum('hbc,chv->bhv', probabilities, value_block, precision=HIGHEST)
    window_mix = lax.map(window_block, jnp.arange(window_count, dtype=jnp.int32)).reshape(length, H, DV)
    combined = linear_normed + window_mix
    mean_squares = lax.optimization_barrier(jnp.mean(combined * combined, axis=(1, 2)))
    output_rows = combined * lax.rsqrt(mean_squares + 1e-06)[:, None, None]
    return output_rows.reshape(length, H * DV)
```

```python
import functools
import math

import jax
import jax.numpy as jnp
from jax import lax
from jax.experimental import pallas as pl
from jax.experimental.pallas import tpu as pltpu
from jax.sharding import PartitionSpec as P

DK = 16
DV = 128
WIN = 64
C = 128
ROWS = 160
MESH = pl.DeviceIdType.MESH
F32 = jnp.float32
BF16 = jnp.bfloat16


def split(value):
    high = value.astype(BF16)
    low = (value - high.astype(F32)).astype(BF16)
    return high, low


def dot(left, right, dims=((1,), (0,))):
    return lax.dot_general(left, right, (dims, ((), ())), preferred_element_type=F32)


def fold(value):
    return value[:, :DV] + value[:, DV:]


def feature_rows(load, pair, linear, constant):
    base = load(0, DK)
    twice = base if pair == 1 else base * pair
    rows = [base * base]
    rows += [twice * load(shift, DK) for shift in range(1, DK // 2)]
    rows += [twice[: DK // 2] * load(DK // 2, DK // 2)]
    rows += [base if linear == 1 else base * linear]
    first = lax.broadcasted_iota(jnp.int32, (8, base.shape[1]), 0) == 0
    rows += [jnp.where(first, F32(constant), F32(0.0))]
    return jnp.concatenate(rows, axis=0)


def kernel(
    seqs, heads,
    qk_hbm, v_hbm, swa_hbm, wqk_ref, wv_ref, gain_ref,
    out_hbm, total_ref,
    xin, vin, qin, kin, xs, xt, us, sx, lin, win, ostage,
    mine, got, prefs, pref, sq, sqgot,
    in_sem, swa_sem, out_sem, hs_sem, hr_sem, s1, r1, s2, r2, s3, r3,
):
    tokens = xs.shape[0]
    local = vin.shape[0]
    chunks = tokens // C
    part = local * ROWS // seqs
    me = lax.axis_index("seq")
    my_head = lax.axis_index("head")

    barrier = pltpu.get_barrier_semaphore()
    for step in range(1, seqs):
        pl.semaphore_signal(barrier, inc=1, device_id={"seq": lax.rem(me + step, seqs)}, device_id_type=MESH)
    for step in range(1, heads):
        pl.semaphore_signal(barrier, inc=1, device_id={"head": lax.rem(my_head + step, heads)}, device_id_type=MESH)

    loads = [pltpu.make_async_copy(qk_hbm, xin.at[pl.ds(8, tokens)], in_sem.at[0])]
    for h in range(local):
        loads.append(pltpu.make_async_copy(
            v_hbm.at[:, pl.ds(h * DV, DV)], vin.at[h, pl.ds(8, tokens)], in_sem.at[1 + h]))
    for load in loads:
        load.start()
    swa_loads = []
    for h in range(local):
        columns = pl.ds(h * DV, DV)
        swa_loads.append(pltpu.make_async_copy(swa_hbm.at[0, :, columns], qin.at[h], swa_sem.at[h, 0]))
        for which in range(2):
            swa_loads.append(pltpu.make_async_copy(
                swa_hbm.at[1 + which, :, columns], kin.at[which, h, pl.ds(WIN, tokens)], swa_sem.at[h, 1 + which]))
    for load in swa_loads:
        load.start()

    pl.semaphore_wait(barrier, seqs - 1 + heads - 1)
    after = {"seq": lax.rem(me + 1, seqs)}

    def remote(source, target, send, receive, device):
        return pltpu.make_async_remote_copy(
            src_ref=source, dst_ref=target, send_sem=send, recv_sem=receive, device_id=device, device_id_type=MESH)

    tail = pl.ds(tokens - 8, 8)
    halos = [remote(qk_hbm.at[tail], xin.at[pl.ds(0, 8)], hs_sem.at[0], hr_sem.at[0], after)]
    for h in range(local):
        halos.append(remote(v_hbm.at[tail, pl.ds(h * DV, DV)], vin.at[h, pl.ds(0, 8)],
                            hs_sem.at[1 + h], hr_sem.at[1 + h], after))
    window_halos = []
    for h in range(local):
        for which in range(2):
            slot = 1 + local + 2 * h + which
            window_halos.append(remote(
                swa_hbm.at[1 + which, pl.ds(tokens - WIN, WIN), pl.ds(h * DV, DV)],
                kin.at[which, h, pl.ds(0, WIN)], hs_sem.at[slot], hr_sem.at[slot], after))
    for copy in halos + window_halos:
        copy.start()

    sx[0] = jnp.zeros(sx.shape[1:], F32)
    for load in loads:
        load.wait()

    def state_step(i, carry):
        c = lax.rem(i + 1, chunks)
        row = pl.multiple_of(c * C, C)

        @pl.when(i == chunks - 1)
        def _():
            for copy in halos:
                copy.wait_recv()
            keep = me > 0
            xin[pl.ds(0, 8)] = jnp.where(keep, xin[pl.ds(0, 8)], 0.0)
            for h in range(local):
                vin[h, pl.ds(0, 8)] = jnp.where(keep, vin[h, pl.ds(0, 8)], 0.0)

        x = wqk_ref[0:1] * xin[pl.ds(row + 6, C)]
        x = x + wqk_ref[1:2] * xin[pl.ds(row + 7, C)]
        x = x + wqk_ref[2:3] * xin[pl.ds(row + 8, C)]
        xs[pl.ds(row, C)] = x
        turned = x.T
        for h in range(local):
            for which in range(2):
                piece = turned[(2 * h + which) * DK:(2 * h + which + 1) * DK]
                xt[c, 2 * h + which, 0:DK] = piece
                xt[c, 2 * h + which, DK:2 * DK] = piece
        again = jnp.where(i < chunks - 1, 1.0, 0.0).astype(F32)
        for h in range(local):
            columns = slice(h * DV, (h + 1) * DV)
            u = wv_ref[0:1, columns] * vin[h, pl.ds(row + 6, C)]
            u = u + wv_ref[1:2, columns] * vin[h, pl.ds(row + 7, C)]
            u = u + wv_ref[2:3, columns] * vin[h, pl.ds(row + 8, C)]
            both = jnp.concatenate(split(u), axis=1)
            us[h, pl.ds(row, C)] = both
            phi = feature_rows(lambda start, size: xt[c, 2 * h + 1, start:start + size], 1, 1, 1.0)
            state = fold(dot(jnp.concatenate(split(phi), axis=1), jnp.concatenate([both, both], axis=0)))
            rows = slice(h * ROWS, (h + 1) * ROWS)
            sx[i + 1, rows] = sx[i, rows] * again + state
        return carry

    lax.fori_loop(0, chunks, state_step, 0)

    mine[...] = sx[chunks - 1] + sx[chunks]
    first = []
    for step in range(1, seqs):
        peer = lax.rem(me + step, seqs)
        rows = pl.ds(pl.multiple_of(peer * part, 8), part)
        first.append(remote(mine.at[rows], got.at[me], s1.at[step - 1], r1.at[step - 1], {"seq": peer}))
        first[-1].start()
    got[me] = mine[pl.ds(pl.multiple_of(me * part, 8), part)]

    lane = lax.broadcasted_iota(jnp.int32, (C, C), 1)
    sub = lax.broadcasted_iota(jnp.int32, (C, C), 0)
    query_lane = lax.rem(lane, 2 * DK) < DK
    causal = lane <= sub

    def local_step(c, carry):
        row = pl.multiple_of(c * C, C)
        x = xs[pl.ds(row, C)]
        left = jnp.concatenate(split(jnp.where(query_lane, x, pltpu.roll(x, DK, 1))), axis=1)
        for pair in range(local // 2):
            sides = []
            for h in (2 * pair, 2 * pair + 1):
                high, low = split(xt[c, 2 * h + 1, 0:DK])
                blank = jnp.zeros((DK, C), BF16)
                pieces = [blank] * (2 * 2 * local)
                pieces[2 * h] = high
                pieces[2 * h + 1] = low
                pieces[2 * local + 2 * h] = high
                sides.append(jnp.concatenate(pieces, axis=0))
            scores = dot(left, jnp.concatenate(sides, axis=1))
            for which in range(2):
                h = 2 * pair + which
                value = scores[:, which * C:(which + 1) * C] + 4.0
                value = jnp.where(causal, value * value + 16.0, 0.0)
                both = us[h, pl.ds(row, C)]
                lin[h, pl.ds(row, C)] = fold(
                    dot(jnp.concatenate(split(value), axis=1), jnp.concatenate([both, both], axis=0)))
        return carry

    lax.fori_loop(0, chunks, local_step, 0)

    for copy in first:
        copy.wait_recv()

    def prefix_step(d, carry):
        prefs[d] = carry
        return carry + got[d]

    lax.fori_loop(0, seqs, prefix_step, jnp.zeros((part, DV), F32))
    own_rows = pl.ds(pl.multiple_of(me * part, 8), part)
    second = []
    for step in range(1, seqs):
        peer = lax.rem(me + step, seqs)
        second.append(remote(prefs.at[peer], pref.at[own_rows], s2.at[step - 1], r2.at[step - 1], {"seq": peer}))
        second[-1].start()
    pref[own_rows] = prefs[me]

    for load in swa_loads:
        load.wait()
    for copy in window_halos:
        copy.wait_recv()
    key = lax.broadcasted_iota(jnp.int32, (WIN, 2 * WIN), 1)
    query = lax.broadcasted_iota(jnp.int32, (WIN, 2 * WIN), 0)
    scale = math.log2(math.e) / math.sqrt(DV)

    def window_step(c, carry):
        row = pl.multiple_of(c * C, C)
        lowest = jnp.where((c == 0) & (me == 0), WIN, 0)
        biases = []
        for b in range(C // WIN):
            low_key = jnp.maximum(query + 1, lowest) if b == 0 else query + 1
            biases.append(jnp.where((key >= low_key) & (key <= query + WIN), 0.0, -1e30).astype(F32))
        for h in range(local):
            q_both = jnp.concatenate(split(qin[h, pl.ds(row, C)] * scale), axis=1)
            k_high, k_low = split(kin[0, h, pl.ds(row, C + WIN)])
            k_high = jnp.concatenate([k_high, k_high], axis=1)
            k_low = jnp.concatenate([k_low, k_low], axis=1)
            v_both = jnp.concatenate(split(kin[1, h, pl.ds(row, C + WIN)]), axis=1)
            for b in range(C // WIN):
                at = slice(b * WIN, b * WIN + 2 * WIN)
                keys = jnp.concatenate([k_high[at], k_low[at]], axis=0)
                scores = fold(dot(q_both[b * WIN:(b + 1) * WIN], keys, ((1,), (1,)))) + biases[b]
                peak = jnp.max(scores, axis=1, keepdims=True)
                weights = jnp.exp2(scores - peak)
                norm = jnp.sum(weights, axis=1, keepdims=True)
                values = jnp.concatenate([v_both[at], v_both[at]], axis=0)
                mixed = fold(dot(jnp.concatenate(split(weights), axis=1), values))
                win[h, pl.ds(row + b * WIN, WIN)] = mixed / norm
        return carry

    lax.fori_loop(0, chunks, window_step, 0)

    for copy in second:
        copy.wait_recv()
    prefs_for = mine

    def carried_step(c, carry):
        row = pl.multiple_of(c * C, C)
        squares = jnp.zeros((C, DV), F32)
        later = jnp.where(c > 0, 1.0, 0.0).astype(F32)
        at = jnp.maximum(c - 1, 0)
        for h in range(local):
            phi_high, phi_low = split(
                feature_rows(lambda start, size: xt[c, 2 * h, start:start + size], 2.0, 8.0, 32.0))
            rows = slice(h * ROWS, (h + 1) * ROWS)
            state = sx[at, rows] + (pref[rows] + sx[chunks, rows] * later)
            both = jnp.concatenate(split(state), axis=1)
            earlier = fold(dot(phi_high, both, ((0,), (0,))) + dot(phi_low, both, ((0,), (0,))))
            mix = lin[h, pl.ds(row, C)] + earlier
            mean = jnp.sum(mix * mix, axis=1, keepdims=True) * (1.0 / DV)
            columns = slice(h * DV, (h + 1) * DV)
            value = mix * lax.rsqrt(mean + 1024.0e-6) * gain_ref[0:1, columns] + win[h, pl.ds(row, C)]
            ostage[pl.ds(row, C), columns] = value
            squares = squares + value * value
        sq[c] = jnp.sum(squares.T, axis=0, keepdims=True)
        pltpu.make_async_copy(ostage.at[pl.ds(row, C)], out_hbm.at[pl.ds(row, C)], out_sem.at[c]).start()
        return carry

    lax.fori_loop(0, chunks, carried_step, 0)

    third = []
    for step in range(1, heads):
        peer = lax.rem(my_head + step, heads)
        third.append(remote(sq, sqgot.at[step - 1], s3.at[step - 1], r3.at[step - 1], {"head": peer}))
        third[-1].start()
    for copy in halos + window_halos + first + second:
        copy.wait_send()

    def out_wait(c, carry):
        row = pl.multiple_of(c * C, C)
        pltpu.make_async_copy(ostage.at[pl.ds(row, C)], out_hbm.at[pl.ds(row, C)], out_sem.at[c]).wait()
        return carry

    lax.fori_loop(0, chunks, out_wait, 0)
    total = sq[...]
    for step, copy in enumerate(third):
        copy.wait_recv()
        total = total + sqgot[step]
    total_ref[...] = total
    for copy in third:
        copy.wait_send()


def per_device(seqs, heads, lin_qk, lin_v, conv_qk, conv_v, swa_qkv, head_gain):
    tokens = lin_qk.shape[0]
    width = lin_v.shape[1]
    local = width // DV
    chunks = tokens // C
    part = local * ROWS // seqs
    hbm = pl.BlockSpec(memory_space=pltpu.HBM)
    vmem = pl.BlockSpec(memory_space=pltpu.VMEM)
    dma = pltpu.SemaphoreType.DMA
    halos = 1 + 3 * local
    combined, squares = pl.pallas_call(
        functools.partial(kernel, seqs, heads),
        out_shape=(
            jax.ShapeDtypeStruct((tokens, width), F32),
            jax.ShapeDtypeStruct((chunks, 1, C), F32),
        ),
        in_specs=[hbm, hbm, hbm, vmem, vmem, vmem],
        out_specs=(hbm, vmem),
        scratch_shapes=[
            pltpu.VMEM((8 + tokens, 2 * DK * local), F32),
            pltpu.VMEM((local, 8 + tokens, DV), F32),
            pltpu.VMEM((local, tokens, DV), F32),
            pltpu.VMEM((2, local, WIN + tokens, DV), F32),
            pltpu.VMEM((tokens, 2 * DK * local), F32),
            pltpu.VMEM((chunks, 2 * local, 2 * DK, C), F32),
            pltpu.VMEM((local, tokens, 2 * DV), BF16),
            pltpu.VMEM((chunks + 1, local * ROWS, DV), F32),
            pltpu.VMEM((local, tokens, DV), F32),
            pltpu.VMEM((local, tokens, DV), F32),
            pltpu.VMEM((tokens, width), F32),
            pltpu.VMEM((local * ROWS, DV), F32),
            pltpu.VMEM((seqs, part, DV), F32),
            pltpu.VMEM((seqs, part, DV), F32),
            pltpu.VMEM((local * ROWS, DV), F32),
            pltpu.VMEM((chunks, 1, C), F32),
            pltpu.VMEM((heads - 1, chunks, 1, C), F32),
            dma((1 + local,)),
            dma((local, 3)),
            dma((chunks,)),
            dma((halos,)),
            dma((halos,)),
            dma((seqs - 1,)),
            dma((seqs - 1,)),
            dma((seqs - 1,)),
            dma((seqs - 1,)),
            dma((heads - 1,)),
            dma((heads - 1,)),
        ],
        compiler_params=pltpu.CompilerParams(
            collective_id=0, has_side_effects=True, vmem_limit_bytes=58 * 1024 * 1024
        ),
        name="mixer",
    )(lin_qk, lin_v, jnp.transpose(swa_qkv, (1, 0, 2)), conv_qk, conv_v, head_gain[None])
    total = squares.reshape(tokens)
    return combined * lax.rsqrt(total / (heads * width) + 1e-06)[:, None]


def solution(mesh):
    placed = (
        P("seq", "head"),
        P("seq", "head"),
        P(None, "head"),
        P(None, "head"),
        P("seq", None, "head"),
        P("head"),
    )
    return jax.shard_map(
        functools.partial(per_device, mesh.shape["seq"], mesh.shape["head"]),
        mesh=mesh, in_specs=placed, out_specs=P("seq", "head"), check_vma=False,
    )
```

```python
import functools
import math

import jax
import jax.numpy as jnp
from jax import lax
from jax.experimental import pallas as pl
from jax.experimental.pallas import tpu as pltpu
from jax.sharding import PartitionSpec as P

DK = 16
DV = 128
WIN = 64
C = 128
QUARTERS = 4
LOCAL_GROUP = 4
WINDOW_GROUP = 16
CARRIED_GROUP = 2
ROWS = 160
MESH = pl.DeviceIdType.MESH
F32 = jnp.float32
BF16 = jnp.bfloat16


def split(value):
    high = value.astype(BF16)
    low = (value - high.astype(F32)).astype(BF16)
    return high, low


def dot(left, right, dims=((1,), (0,))):
    return lax.dot_general(left, right, (dims, ((), ())), preferred_element_type=F32)


def fold(value):
    return value[:, :DV] + value[:, DV:]


def feature_rows(load, pair, linear, constant):
    base = load(0, DK)
    twice = base if pair == 1 else base * pair
    rows = [base * base]
    rows += [twice * load(shift, DK) for shift in range(1, DK // 2)]
    rows += [twice[: DK // 2] * load(DK // 2, DK // 2)]
    rows += [base if linear == 1 else base * linear]
    first = lax.broadcasted_iota(jnp.int32, (8, base.shape[1]), 0) == 0
    rows += [jnp.where(first, F32(constant), F32(0.0))]
    return jnp.concatenate(rows, axis=0)


def kernel(
    seqs, heads,
    qk_hbm, v_hbm, swa_hbm, wqk_ref, wv_ref, gain_ref,
    out_ref, total_ref,
    xin, vin, qin, kin, xs, xt, us, sx, lin, win,
    mine, got, prefs, pref, sq, sqgot,
    in_sem, swa_sem, hs_sem, hr_sem, s1, r1, s2, r2, s3, r3,
):
    tokens = xs.shape[0]
    local = vin.shape[0]
    chunks = tokens // C
    part = local * ROWS // seqs
    quarter = tokens // QUARTERS
    me = lax.axis_index("seq")
    my_head = lax.axis_index("head")

    def lin_loads(n):
        at = pl.multiple_of(n * quarter, 8)
        copies = [pltpu.make_async_copy(
            qk_hbm.at[pl.ds(at, quarter)], xin.at[pl.ds(8 + at, quarter)], in_sem.at[n, 0])]
        for h in range(local):
            copies.append(pltpu.make_async_copy(
                v_hbm.at[pl.ds(at, quarter), pl.ds(h * DV, DV)], vin.at[h, pl.ds(8 + at, quarter)],
                in_sem.at[n, 1 + h]))
        return copies

    for n in range(QUARTERS):
        for load in lin_loads(n):
            load.start()

    barrier = pltpu.get_barrier_semaphore()
    for step in range(1, seqs):
        pl.semaphore_signal(barrier, inc=1, device_id={"seq": lax.rem(me + step, seqs)}, device_id_type=MESH)
    for step in range(1, heads):
        pl.semaphore_signal(barrier, inc=1, device_id={"head": lax.rem(my_head + step, heads)}, device_id_type=MESH)

    swa_loads = []
    for h in range(local):
        columns = pl.ds(h * DV, DV)
        swa_loads.append(pltpu.make_async_copy(swa_hbm.at[0, :, columns], qin.at[h], swa_sem.at[h, 0]))
        for which in range(2):
            swa_loads.append(pltpu.make_async_copy(
                swa_hbm.at[1 + which, :, columns], kin.at[which, h, pl.ds(WIN, tokens)], swa_sem.at[h, 1 + which]))

    pl.semaphore_wait(barrier, seqs - 1 + heads - 1)
    after = {"seq": lax.rem(me + 1, seqs)}

    def remote(source, target, send, receive, device):
        return pltpu.make_async_remote_copy(
            src_ref=source, dst_ref=target, send_sem=send, recv_sem=receive, device_id=device, device_id_type=MESH)

    tail = pl.ds(tokens - 8, 8)
    halos = [remote(qk_hbm.at[tail], xin.at[pl.ds(0, 8)], hs_sem.at[0], hr_sem.at[0], after)]
    for h in range(local):
        halos.append(remote(v_hbm.at[tail, pl.ds(h * DV, DV)], vin.at[h, pl.ds(0, 8)],
                            hs_sem.at[1 + h], hr_sem.at[1 + h], after))
    window_halos = []
    for h in range(local):
        for which in range(2):
            slot = 1 + local + 2 * h + which
            window_halos.append(remote(
                swa_hbm.at[1 + which, pl.ds(tokens - WIN, WIN), pl.ds(h * DV, DV)],
                kin.at[which, h, pl.ds(0, WIN)], hs_sem.at[slot], hr_sem.at[slot], after))
    for copy in halos:
        copy.start()

    sx[0] = jnp.zeros(sx.shape[1:], F32)
    for load in lin_loads(0):
        load.wait()
    per_quarter = chunks // QUARTERS
    steps = chunks // 2

    def state_step(i, carry):
        last = i == steps - 1

        @pl.when((lax.rem(2 * i + 2, per_quarter) == 0) & jnp.logical_not(last))
        def _():
            for load in lin_loads((2 * i + 2) // per_quarter):
                load.wait()

        @pl.when(last)
        def _():
            for copy in halos:
                copy.wait_recv()
            keep = me > 0
            xin[pl.ds(0, 8)] = jnp.where(keep, xin[pl.ds(0, 8)], 0.0)
            for h in range(local):
                vin[h, pl.ds(0, 8)] = jnp.where(keep, vin[h, pl.ds(0, 8)], 0.0)

        which_chunks = (2 * i + 1, lax.rem(2 * i + 2, chunks))
        pairs = [(c, h) for c in range(2) for h in range(local)]
        turned = []
        for c in which_chunks:
            row = pl.multiple_of(c * C, C)
            x = wqk_ref[0:1] * xin[pl.ds(row + 6, C)]
            x = x + wqk_ref[1:2] * xin[pl.ds(row + 7, C)]
            x = x + wqk_ref[2:3] * xin[pl.ds(row + 8, C)]
            xs[pl.ds(row, C)] = x
            turned.append(x.T)
        boths = []
        for n, h in pairs:
            row = pl.multiple_of(which_chunks[n] * C, C)
            columns = slice(h * DV, (h + 1) * DV)
            u = wv_ref[0:1, columns] * vin[h, pl.ds(row + 6, C)]
            u = u + wv_ref[1:2, columns] * vin[h, pl.ds(row + 7, C)]
            u = u + wv_ref[2:3, columns] * vin[h, pl.ds(row + 8, C)]
            both = jnp.concatenate(split(u), axis=1)
            us[h, pl.ds(row, C)] = both
            boths.append(both)
        for c, value in zip(which_chunks, turned):
            for piece in range(2 * local):
                at = value[piece * DK:(piece + 1) * DK]
                xt[c, piece, 0:DK] = at
                xt[c, piece, DK:2 * DK] = at
        phis = []
        for n, h in pairs:
            c = which_chunks[n]
            phi = feature_rows(lambda start, size: xt[c, 2 * h + 1, start:start + size], 1, 1, 1.0)
            phis.append(jnp.concatenate(split(phi), axis=1))
        states = [dot(phi, jnp.concatenate([both, both], axis=0)) for phi, both in zip(phis, boths)]
        again = jnp.where(last, 0.0, 1.0).astype(F32)
        for h in range(local):
            rows = slice(h * ROWS, (h + 1) * ROWS)
            total = sx[2 * i, rows] + fold(states[h])
            sx[2 * i + 1, rows] = total
            sx[2 * i + 2, rows] = total * again + fold(states[local + h])
        return carry

    lax.fori_loop(0, steps, state_step, 0)

    mine[...] = sx[chunks - 1] + sx[chunks]
    first = []
    for step in range(1, seqs):
        peer = lax.rem(me + step, seqs)
        rows = pl.ds(pl.multiple_of(peer * part, 8), part)
        first.append(remote(mine.at[rows], got.at[me], s1.at[step - 1], r1.at[step - 1], {"seq": peer}))
        first[-1].start()
    got[me] = mine[pl.ds(pl.multiple_of(me * part, 8), part)]
    for copy in window_halos:
        copy.start()
    for load in swa_loads:
        load.start()

    lane = lax.broadcasted_iota(jnp.int32, (C, C), 1)
    sub = lax.broadcasted_iota(jnp.int32, (C, C), 0)
    query_lane = lax.rem(lane, 2 * DK) < DK
    causal = lane <= sub

    def local_step(i, carry):
        which_chunks = [LOCAL_GROUP * i + n for n in range(LOCAL_GROUP)]
        at_rows = [pl.ds(pl.multiple_of(c * C, C), C) for c in which_chunks]
        lefts = []
        for rows in at_rows:
            x = xs[rows]
            lefts.append(jnp.concatenate(split(jnp.where(query_lane, x, pltpu.roll(x, DK, 1))), axis=1))
        rights = []
        for c in which_chunks:
            for pair in range(local // 2):
                sides = []
                for h in (2 * pair, 2 * pair + 1):
                    high, low = split(xt[c, 2 * h + 1, 0:DK])
                    blank = jnp.zeros((DK, C), BF16)
                    pieces = [blank] * (2 * 2 * local)
                    pieces[2 * h] = high
                    pieces[2 * h + 1] = low
                    pieces[2 * local + 2 * h] = high
                    sides.append(jnp.concatenate(pieces, axis=0))
                rights.append(jnp.concatenate(sides, axis=1))
        scores = [dot(lefts[n], rights[n * (local // 2) + pair])
                  for n in range(LOCAL_GROUP) for pair in range(local // 2)]
        values = []
        for score in scores:
            for which in range(2):
                value = score[:, which * C:(which + 1) * C] + 4.0
                value = jnp.where(causal, value * value + 16.0, 0.0)
                values.append(jnp.concatenate(split(value), axis=1))
        sums = []
        for n in range(LOCAL_GROUP):
            for h in range(local):
                both = us[h, at_rows[n]]
                sums.append(dot(values[n * local + h], jnp.concatenate([both, both], axis=0)))
        for n in range(LOCAL_GROUP):
            for h in range(local):
                lin[h, at_rows[n]] = fold(sums[n * local + h])
        return carry

    lax.fori_loop(0, chunks // LOCAL_GROUP, local_step, 0)

    for copy in first:
        copy.wait_recv()

    def prefix_step(d, carry):
        prefs[d] = carry
        return carry + got[d]

    lax.fori_loop(0, seqs, prefix_step, jnp.zeros((part, DV), F32))
    own_rows = pl.ds(pl.multiple_of(me * part, 8), part)
    second = []
    for step in range(1, seqs):
        peer = lax.rem(me + step, seqs)
        second.append(remote(prefs.at[peer], pref.at[own_rows], s2.at[step - 1], r2.at[step - 1], {"seq": peer}))
        second[-1].start()
    pref[own_rows] = prefs[me]

    for load in swa_loads:
        load.wait()
    for copy in window_halos:
        copy.wait_recv()
    key = lax.broadcasted_iota(jnp.int32, (WIN, C), 1)
    query = lax.broadcasted_iota(jnp.int32, (WIN, C), 0)
    scale = math.log2(math.e) / math.sqrt(DV)
    own_half = lax.rem(lax.broadcasted_iota(jnp.int32, (C, 2 * C), 1), C) < WIN
    inside = ((key < WIN) & (key <= query)) | ((key >= WIN) & (key - C > query - WIN))
    lowest = jnp.where(me == 0, C, 0)
    starts = inside & ((key < WIN) | (key >= lowest))
    bias_first = jnp.where(starts, 0.0, -1e30).astype(F32)
    bias_even = jnp.where(inside, 0.0, -1e30).astype(F32)
    bias_odd = jnp.where((key <= query + WIN) & (key > query), 0.0, -1e30).astype(F32)

    def window_step(i, carry):
        h = i // (chunks // WINDOW_GROUP)
        g = lax.rem(i, chunks // WINDOW_GROUP)
        base = pl.multiple_of(g * (WINDOW_GROUP * C), C)

        def rows_of(which, j):
            return kin[which, h, pl.ds(base + j * WIN, WIN)]

        tiles = [jnp.concatenate(split(kin[0, h, pl.ds(base + WIN + j * C, C)].T), axis=1)
                 for j in range(WINDOW_GROUP)]
        ring = jnp.concatenate(split(jnp.concatenate([rows_of(0, 1), rows_of(0, 0)], axis=0).T), axis=1)
        opening = jnp.where(g == 0, bias_first, bias_even)
        scores = []
        for j in range(WINDOW_GROUP):
            own = tiles[j]
            if j > 0:
                ring = jnp.where(own_half, own, tiles[j - 1])
            q_both = jnp.concatenate(split(qin[h, pl.ds(base + j * C, C)] * scale), axis=1)
            scores.append(fold(dot(q_both[:WIN], jnp.concatenate([ring, ring], axis=0)))
                          + (opening if j == 0 else bias_even))
            scores.append(fold(dot(q_both[WIN:], jnp.concatenate([own, own], axis=0))) + bias_odd)
        weights = []
        for score in scores:
            weight = jnp.exp2(score - jnp.max(score, axis=1, keepdims=True))
            weights.append((jnp.concatenate(split(weight), axis=1), jnp.sum(weight, axis=1, keepdims=True)))
        values = [jnp.concatenate(split(rows_of(1, j)), axis=1) for j in range(2 * WINDOW_GROUP + 1)]
        for j, (weight, norm) in enumerate(weights):
            even = j if j % 2 else j + 1
            odd = j + 1 if j % 2 else j
            tile = [values[even], values[odd]]
            win[h, pl.ds(base + j * WIN, WIN)] = fold(dot(weight, jnp.concatenate(tile + tile, axis=0))) / norm
        return carry

    lax.fori_loop(0, local * chunks // WINDOW_GROUP, window_step, 0)

    for copy in second:
        copy.wait_recv()

    def carried_step(i, carry):
        which_chunks = [CARRIED_GROUP * i + n for n in range(CARRIED_GROUP)]
        at_rows = [pl.ds(pl.multiple_of(c * C, C), C) for c in which_chunks]
        pairs = [(n, h) for n in range(CARRIED_GROUP) for h in range(local)]
        phis = []
        for n, h in pairs:
            phi = feature_rows(
                lambda start, size: xt[which_chunks[n], 2 * h, start:start + size], 2.0, 8.0, 32.0)
            phis.append(jnp.concatenate(split(phi), axis=0).T)
        states = []
        for n, h in pairs:
            c = which_chunks[n]
            rows = slice(h * ROWS, (h + 1) * ROWS)
            later = jnp.where(c > 0, 1.0, 0.0).astype(F32)
            state = sx[jnp.maximum(c - 1, 0), rows] + (pref[rows] + sx[chunks, rows] * later)
            both = jnp.concatenate(split(state), axis=1)
            states.append(jnp.concatenate([both, both], axis=0))
        earlier = [dot(phi, state) for phi, state in zip(phis, states)]
        mixes = [lin[h, at_rows[n]] + fold(earlier[n * local + h]) for n, h in pairs]
        means = [jnp.sum(mix * mix, axis=1, keepdims=True) * (1.0 / DV) for mix in mixes]
        squares = [jnp.zeros((C, DV), F32) for _ in which_chunks]
        for (n, h), mix, mean in zip(pairs, mixes, means):
            columns = slice(h * DV, (h + 1) * DV)
            value = mix * lax.rsqrt(mean + 1024.0e-6) * gain_ref[0:1, columns] + win[h, at_rows[n]]
            out_ref[at_rows[n], columns] = value
            squares[n] = squares[n] + value * value
        for c, square in zip(which_chunks, squares):
            sq[c] = jnp.sum(square.T, axis=0, keepdims=True)
        return carry

    lax.fori_loop(0, chunks // CARRIED_GROUP, carried_step, 0)

    third = []
    for step in range(1, heads):
        peer = lax.rem(my_head + step, heads)
        third.append(remote(sq, sqgot.at[step - 1], s3.at[step - 1], r3.at[step - 1], {"head": peer}))
        third[-1].start()
    for copy in halos + window_halos + first + second:
        copy.wait_send()
    total = sq[...]
    for step, copy in enumerate(third):
        copy.wait_recv()
        total = total + sqgot[step]
    total_ref[...] = total
    for copy in third:
        copy.wait_send()


def scale_kernel(count, value_ref, total_ref, out_hbm, stage, sems):
    chunks, width = total_ref.shape[0], value_ref.shape[1]
    copies = []
    for c in range(chunks):
        rows = pl.ds(c * C, C)
        factor = lax.rsqrt(total_ref[c] * (1.0 / count) + 1e-06)
        factor = jnp.broadcast_to(factor, (C, C)).T
        for h in range(width // DV):
            columns = slice(h * DV, (h + 1) * DV)
            stage[rows, columns] = value_ref[rows, columns] * factor
        copies.append(pltpu.make_async_copy(stage.at[rows], out_hbm.at[rows], sems.at[c]))
        copies[-1].start()
    for copy in copies:
        copy.wait()


def per_device(seqs, heads, lin_qk, lin_v, conv_qk, conv_v, swa_qkv, head_gain):
    tokens = lin_qk.shape[0]
    width = lin_v.shape[1]
    local = width // DV
    chunks = tokens // C
    part = local * ROWS // seqs
    hbm = pl.BlockSpec(memory_space=pltpu.HBM)
    vmem = pl.BlockSpec(memory_space=pltpu.VMEM)
    dma = pltpu.SemaphoreType.DMA
    halos = 1 + 3 * local
    combined, squares = pl.pallas_call(
        functools.partial(kernel, seqs, heads),
        out_shape=(
            jax.ShapeDtypeStruct((tokens, width), F32),
            jax.ShapeDtypeStruct((chunks, 1, C), F32),
        ),
        in_specs=[hbm, hbm, hbm, vmem, vmem, vmem],
        out_specs=(vmem, vmem),
        scratch_shapes=[
            pltpu.VMEM((8 + tokens, 2 * DK * local), F32),
            pltpu.VMEM((local, 8 + tokens, DV), F32),
            pltpu.VMEM((local, tokens, DV), F32),
            pltpu.VMEM((2, local, WIN + tokens, DV), F32),
            pltpu.VMEM((tokens, 2 * DK * local), F32),
            pltpu.VMEM((chunks, 2 * local, 2 * DK, C), F32),
            pltpu.VMEM((local, tokens, 2 * DV), BF16),
            pltpu.VMEM((chunks + 1, local * ROWS, DV), F32),
            pltpu.VMEM((local, tokens, DV), F32),
            pltpu.VMEM((local, tokens, DV), F32),
            pltpu.VMEM((local * ROWS, DV), F32),
            pltpu.VMEM((seqs, part, DV), F32),
            pltpu.VMEM((seqs, part, DV), F32),
            pltpu.VMEM((local * ROWS, DV), F32),
            pltpu.VMEM((chunks, 1, C), F32),
            pltpu.VMEM((heads - 1, chunks, 1, C), F32),
            dma((QUARTERS, 1 + local)),
            dma((local, 3)),
            dma((halos,)),
            dma((halos,)),
            dma((seqs - 1,)),
            dma((seqs - 1,)),
            dma((seqs - 1,)),
            dma((seqs - 1,)),
            dma((heads - 1,)),
            dma((heads - 1,)),
        ],
        compiler_params=pltpu.CompilerParams(
            collective_id=0, has_side_effects=True, vmem_limit_bytes=48 * 1024 * 1024
        ),
        name="mixer",
    )(lin_qk, lin_v, jnp.transpose(swa_qkv, (1, 0, 2)), conv_qk, conv_v, head_gain[None])
    return pl.pallas_call(
        functools.partial(scale_kernel, heads * width),
        out_shape=jax.ShapeDtypeStruct((tokens, width), F32),
        in_specs=[vmem, vmem],
        out_specs=hbm,
        scratch_shapes=[pltpu.VMEM((tokens, width), F32), dma((chunks,))],
        compiler_params=pltpu.CompilerParams(vmem_limit_bytes=16 * 1024 * 1024),
        name="scale",
    )(combined, squares)


def solution(mesh):
    placed = (
        P("seq", "head"),
        P("seq", "head"),
        P(None, "head"),
        P(None, "head"),
        P("seq", None, "head"),
        P("head"),
    )
    return jax.shard_map(
        functools.partial(per_device, mesh.shape["seq"], mesh.shape["head"]),
        mesh=mesh, in_specs=placed, out_specs=P("seq", "head"), check_vma=False,
    )
```

```python
import functools
import math

import jax
import jax.numpy as jnp
from jax import lax
from jax.experimental import pallas as pl
from jax.experimental.pallas import tpu as pltpu
from jax.sharding import PartitionSpec as P

DK = 16
DV = 128
WIN = 64
C = 128
QUARTERS = 4
LOCAL_GROUP = 4
WINDOW_GROUP = 16
CARRIED_GROUP = 4
PREFIX_HEAD = 1
ROWS = 160
MESH = pl.DeviceIdType.MESH
F32 = jnp.float32
BF16 = jnp.bfloat16


def split(value):
    high = value.astype(BF16)
    low = (value - high.astype(F32)).astype(BF16)
    return high, low


def dot(left, right, dims=((1,), (0,))):
    return lax.dot_general(left, right, (dims, ((), ())), preferred_element_type=F32)


def fold(value):
    return value[:, :DV] + value[:, DV:]


def feature_rows(load, pair, linear, constant):
    base = load(0, DK)
    twice = base if pair == 1 else base * pair
    rows = [base * base]
    rows += [twice * load(shift, DK) for shift in range(1, DK // 2)]
    rows += [twice[: DK // 2] * load(DK // 2, DK // 2)]
    rows += [base if linear == 1 else base * linear]
    first = lax.broadcasted_iota(jnp.int32, (8, base.shape[1]), 0) == 0
    rows += [jnp.where(first, F32(constant), F32(0.0))]
    return jnp.concatenate(rows, axis=0)


def kernel(
    seqs, heads,
    qk_hbm, v_hbm, swa_hbm, wqk_ref, wv_ref, gain_ref,
    out_ref, total_ref,
    xin, vin, qin, kin, xs, xt, us, sx, lin, win,
    mine, got, prefs, pref, sq, sqgot,
    in_sem, swa_sem, hs_sem, hr_sem, s1, r1, s2, r2, s3, r3,
):
    tokens = xs.shape[0]
    local = vin.shape[0]
    chunks = tokens // C
    part = local * ROWS // seqs
    quarter = tokens // QUARTERS
    me = lax.axis_index("seq")
    my_head = lax.axis_index("head")

    def lin_loads(n):
        at = pl.multiple_of(n * quarter, 8)
        copies = [pltpu.make_async_copy(
            qk_hbm.at[pl.ds(at, quarter)], xin.at[pl.ds(8 + at, quarter)], in_sem.at[n, 0])]
        for h in range(local):
            copies.append(pltpu.make_async_copy(
                v_hbm.at[pl.ds(at, quarter), pl.ds(h * DV, DV)], vin.at[h, pl.ds(8 + at, quarter)],
                in_sem.at[n, 1 + h]))
        return copies

    for n in range(QUARTERS):
        for load in lin_loads(n):
            load.start()

    barrier = pltpu.get_barrier_semaphore()
    for step in range(1, seqs):
        pl.semaphore_signal(barrier, inc=1, device_id={"seq": lax.rem(me + step, seqs)}, device_id_type=MESH)
    for step in range(1, heads):
        pl.semaphore_signal(barrier, inc=1, device_id={"head": lax.rem(my_head + step, heads)}, device_id_type=MESH)

    def head_loads(h):
        columns = pl.ds(pl.multiple_of(h * DV, DV), DV)
        copies = [pltpu.make_async_copy(swa_hbm.at[0, :, columns], qin.at[h], swa_sem.at[h, 0])]
        for which in range(2):
            copies.append(pltpu.make_async_copy(
                swa_hbm.at[1 + which, :, columns], kin.at[which, h, pl.ds(WIN, tokens)], swa_sem.at[h, 1 + which]))
        return copies

    for h in range(local):
        for load in head_loads(h):
            load.start()
    after = {"seq": lax.rem(me + 1, seqs)}

    def remote(source, target, send, receive, device):
        return pltpu.make_async_remote_copy(
            src_ref=source, dst_ref=target, send_sem=send, recv_sem=receive, device_id=device, device_id_type=MESH)

    tail = pl.ds(tokens - 8, 8)
    halos = [remote(qk_hbm.at[tail], xin.at[pl.ds(0, 8)], hs_sem.at[0], hr_sem.at[0], after)]
    for h in range(local):
        halos.append(remote(v_hbm.at[tail, pl.ds(h * DV, DV)], vin.at[h, pl.ds(0, 8)],
                            hs_sem.at[1 + h], hr_sem.at[1 + h], after))
    window_halos = []
    for h in range(local):
        for which in range(2):
            slot = 1 + local + 2 * h + which
            window_halos.append(remote(
                swa_hbm.at[1 + which, pl.ds(tokens - WIN, WIN), pl.ds(h * DV, DV)],
                kin.at[which, h, pl.ds(0, WIN)], hs_sem.at[slot], hr_sem.at[slot], after))

    sx[0] = jnp.zeros(sx.shape[1:], F32)
    for load in lin_loads(0):
        load.wait()
    per_quarter = chunks // QUARTERS
    steps = chunks // 2

    def state_step(i, carry):
        last = i == steps - 1

        @pl.when((lax.rem(2 * i + 2, per_quarter) == 0) & jnp.logical_not(last))
        def _():
            for load in lin_loads((2 * i + 2) // per_quarter):
                load.wait()

        @pl.when(i == 1)
        def _():
            pl.semaphore_wait(barrier, seqs - 1 + heads - 1)
            for copy in halos + window_halos:
                copy.start()

        @pl.when(last)
        def _():
            for copy in halos:
                copy.wait_recv()
            keep = me > 0
            xin[pl.ds(0, 8)] = jnp.where(keep, xin[pl.ds(0, 8)], 0.0)
            for h in range(local):
                vin[h, pl.ds(0, 8)] = jnp.where(keep, vin[h, pl.ds(0, 8)], 0.0)

        which_chunks = (2 * i + 1, lax.rem(2 * i + 2, chunks))
        pairs = [(c, h) for c in range(2) for h in range(local)]
        turned = []
        for c in which_chunks:
            row = pl.multiple_of(c * C, C)
            x = wqk_ref[0:1] * xin[pl.ds(row + 6, C)]
            x = x + wqk_ref[1:2] * xin[pl.ds(row + 7, C)]
            x = x + wqk_ref[2:3] * xin[pl.ds(row + 8, C)]
            xs[pl.ds(row, C)] = x
            turned.append(x.T)
        boths = []
        for n, h in pairs:
            row = pl.multiple_of(which_chunks[n] * C, C)
            columns = slice(h * DV, (h + 1) * DV)
            u = wv_ref[0:1, columns] * vin[h, pl.ds(row + 6, C)]
            u = u + wv_ref[1:2, columns] * vin[h, pl.ds(row + 7, C)]
            u = u + wv_ref[2:3, columns] * vin[h, pl.ds(row + 8, C)]
            both = jnp.concatenate(split(u), axis=1)
            us[h, pl.ds(row, C)] = both
            boths.append(both)
        for c, value in zip(which_chunks, turned):
            for piece in range(2 * local):
                at = value[piece * DK:(piece + 1) * DK]
                xt[c, piece, 0:DK] = at
                xt[c, piece, DK:2 * DK] = at
        phis = []
        for n, h in pairs:
            c = which_chunks[n]
            phi = feature_rows(lambda start, size: xt[c, 2 * h + 1, start:start + size], 1, 1, 1.0)
            phis.append(jnp.concatenate(split(phi), axis=1))
        states = [dot(phi, jnp.concatenate([both, both], axis=0)) for phi, both in zip(phis, boths)]
        again = jnp.where(last, 0.0, 1.0).astype(F32)
        for h in range(local):
            rows = slice(h * ROWS, (h + 1) * ROWS)
            total = sx[2 * i, rows] + fold(states[h])
            sx[2 * i + 1, rows] = total
            sx[2 * i + 2, rows] = total * again + fold(states[local + h])
        return carry

    lax.fori_loop(0, steps, state_step, 0)

    mine[...] = sx[chunks - 1] + sx[chunks]
    first = []
    for step in range(1, seqs):
        peer = lax.rem(me + step, seqs)
        rows = pl.ds(pl.multiple_of(peer * part, 8), part)
        first.append(remote(mine.at[rows], got.at[me], s1.at[step - 1], r1.at[step - 1], {"seq": peer}))
        first[-1].start()
    got[me] = mine[pl.ds(pl.multiple_of(me * part, 8), part)]

    lane = lax.broadcasted_iota(jnp.int32, (C, C), 1)
    sub = lax.broadcasted_iota(jnp.int32, (C, C), 0)
    query_lane = lax.rem(lane, 2 * DK) < DK
    causal = lane <= sub

    def local_step(i, carry):
        which_chunks = [LOCAL_GROUP * i + n for n in range(LOCAL_GROUP)]
        at_rows = [pl.ds(pl.multiple_of(c * C, C), C) for c in which_chunks]
        lefts = []
        for rows in at_rows:
            x = xs[rows]
            lefts.append(jnp.concatenate(split(jnp.where(query_lane, x, pltpu.roll(x, DK, 1))), axis=1))
        rights = []
        for c in which_chunks:
            for pair in range(local // 2):
                sides = []
                for h in (2 * pair, 2 * pair + 1):
                    high, low = split(xt[c, 2 * h + 1, 0:DK])
                    blank = jnp.zeros((DK, C), BF16)
                    pieces = [blank] * (2 * 2 * local)
                    pieces[2 * h] = high
                    pieces[2 * h + 1] = low
                    pieces[2 * local + 2 * h] = high
                    sides.append(jnp.concatenate(pieces, axis=0))
                rights.append(jnp.concatenate(sides, axis=1))
        scores = [dot(lefts[n], rights[n * (local // 2) + pair])
                  for n in range(LOCAL_GROUP) for pair in range(local // 2)]
        values = []
        for score in scores:
            for which in range(2):
                value = score[:, which * C:(which + 1) * C] + 4.0
                value = jnp.where(causal, value * value + 16.0, 0.0)
                values.append(jnp.concatenate(split(value), axis=1))
        sums = []
        for n in range(LOCAL_GROUP):
            for h in range(local):
                both = us[h, at_rows[n]]
                sums.append(dot(values[n * local + h], jnp.concatenate([both, both], axis=0)))
        for n in range(LOCAL_GROUP):
            for h in range(local):
                lin[h, at_rows[n]] = fold(sums[n * local + h])
        return carry

    lax.fori_loop(0, chunks // LOCAL_GROUP, local_step, 0)

    own_rows = pl.ds(pl.multiple_of(me * part, 8), part)
    second = []
    for step in range(1, seqs):
        peer = lax.rem(me + step, seqs)
        second.append(remote(prefs.at[peer], pref.at[own_rows], s2.at[step - 1], r2.at[step - 1], {"seq": peer}))

    def prefix_step(d, carry):
        prefs[d] = carry
        return carry + got[d]

    for copy in window_halos:
        copy.wait_recv()
    key = lax.broadcasted_iota(jnp.int32, (WIN, C), 1)
    query = lax.broadcasted_iota(jnp.int32, (WIN, C), 0)
    scale = math.log2(math.e) / math.sqrt(DV)
    own_half = lax.rem(lax.broadcasted_iota(jnp.int32, (C, 2 * C), 1), C) < WIN
    inside = ((key < WIN) & (key <= query)) | ((key >= WIN) & (key - C > query - WIN))
    lowest = jnp.where(me == 0, C, 0)
    starts = inside & ((key < WIN) | (key >= lowest))
    bias_first = jnp.where(starts, 0.0, -1e30).astype(F32)
    bias_even = jnp.where(inside, 0.0, -1e30).astype(F32)
    bias_odd = jnp.where((key <= query + WIN) & (key > query), 0.0, -1e30).astype(F32)

    def window_step(i, carry):
        h = i // (chunks // WINDOW_GROUP)
        g = lax.rem(i, chunks // WINDOW_GROUP)
        base = pl.multiple_of(g * (WINDOW_GROUP * C), C)

        @pl.when((h == PREFIX_HEAD) & (g == 0))
        def _():
            for copy in first:
                copy.wait_recv()
            lax.fori_loop(0, seqs, prefix_step, jnp.zeros((part, DV), F32))
            for copy in second:
                copy.start()
            pref[own_rows] = prefs[me]

        @pl.when(g == 0)
        def _():
            for load in head_loads(h):
                load.wait()

        def rows_of(which, j):
            return kin[which, h, pl.ds(base + j * WIN, WIN)]

        tiles = [jnp.concatenate(split(kin[0, h, pl.ds(base + WIN + j * C, C)].T), axis=1)
                 for j in range(WINDOW_GROUP)]
        ring = jnp.concatenate(split(jnp.concatenate([rows_of(0, 1), rows_of(0, 0)], axis=0).T), axis=1)
        opening = jnp.where(g == 0, bias_first, bias_even)
        scores = []
        for j in range(WINDOW_GROUP):
            own = tiles[j]
            if j > 0:
                ring = jnp.where(own_half, own, tiles[j - 1])
            q_both = jnp.concatenate(split(qin[h, pl.ds(base + j * C, C)] * scale), axis=1)
            scores.append(fold(dot(q_both[:WIN], jnp.concatenate([ring, ring], axis=0)))
                          + (opening if j == 0 else bias_even))
            scores.append(fold(dot(q_both[WIN:], jnp.concatenate([own, own], axis=0))) + bias_odd)
        weights = []
        for score in scores:
            weight = jnp.exp2(score - jnp.max(score, axis=1, keepdims=True))
            weights.append((jnp.concatenate(split(weight), axis=1), jnp.sum(weight, axis=1, keepdims=True)))
        values = [jnp.concatenate(split(rows_of(1, j)), axis=1) for j in range(2 * WINDOW_GROUP + 1)]
        for j, (weight, norm) in enumerate(weights):
            even = j if j % 2 else j + 1
            odd = j + 1 if j % 2 else j
            tile = [values[even], values[odd]]
            win[h, pl.ds(base + j * WIN, WIN)] = fold(dot(weight, jnp.concatenate(tile + tile, axis=0))) / norm
        return carry

    lax.fori_loop(0, local * chunks // WINDOW_GROUP, window_step, 0)

    for copy in second:
        copy.wait_recv()

    def carried_step(i, carry):
        which_chunks = [CARRIED_GROUP * i + n for n in range(CARRIED_GROUP)]
        at_rows = [pl.ds(pl.multiple_of(c * C, C), C) for c in which_chunks]
        pairs = [(n, h) for n in range(CARRIED_GROUP) for h in range(local)]
        phis = []
        for n, h in pairs:
            phi = feature_rows(
                lambda start, size: xt[which_chunks[n], 2 * h, start:start + size], 2.0, 8.0, 32.0)
            phis.append(jnp.concatenate(split(phi), axis=0).T)
        states = []
        for n, h in pairs:
            c = which_chunks[n]
            rows = slice(h * ROWS, (h + 1) * ROWS)
            later = jnp.where(c > 0, 1.0, 0.0).astype(F32)
            state = sx[jnp.maximum(c - 1, 0), rows] + (pref[rows] + sx[chunks, rows] * later)
            both = jnp.concatenate(split(state), axis=1)
            states.append(jnp.concatenate([both, both], axis=0))
        earlier = [dot(phi, state) for phi, state in zip(phis, states)]
        mixes = [lin[h, at_rows[n]] + fold(earlier[n * local + h]) for n, h in pairs]
        means = [jnp.sum(mix * mix, axis=1, keepdims=True) * (1.0 / DV) for mix in mixes]
        squares = [jnp.zeros((C, DV), F32) for _ in which_chunks]
        for (n, h), mix, mean in zip(pairs, mixes, means):
            columns = slice(h * DV, (h + 1) * DV)
            value = mix * lax.rsqrt(mean + 1024.0e-6) * gain_ref[0:1, columns] + win[h, at_rows[n]]
            out_ref[at_rows[n], columns] = value
            squares[n] = squares[n] + value * value
        for c, square in zip(which_chunks, squares):
            sq[c] = jnp.sum(square.T, axis=0, keepdims=True)
        return carry

    lax.fori_loop(0, chunks // CARRIED_GROUP, carried_step, 0)

    third = []
    for step in range(1, heads):
        peer = lax.rem(my_head + step, heads)
        third.append(remote(sq, sqgot.at[step - 1], s3.at[step - 1], r3.at[step - 1], {"head": peer}))
        third[-1].start()
    for copy in halos + window_halos + first + second:
        copy.wait_send()
    total = sq[...]
    for step, copy in enumerate(third):
        copy.wait_recv()
        total = total + sqgot[step]
    total_ref[...] = total
    for copy in third:
        copy.wait_send()


def scale_kernel(count, value_ref, total_ref, out_hbm, stage, sems):
    chunks, width = total_ref.shape[0], value_ref.shape[1]
    copies = []
    for c in range(chunks):
        rows = pl.ds(c * C, C)
        factor = lax.rsqrt(total_ref[c] * (1.0 / count) + 1e-06)
        factor = jnp.broadcast_to(factor, (C, C)).T
        for h in range(width // DV):
            columns = slice(h * DV, (h + 1) * DV)
            stage[rows, columns] = value_ref[rows, columns] * factor
        copies.append(pltpu.make_async_copy(stage.at[rows], out_hbm.at[rows], sems.at[c]))
        copies[-1].start()
    for copy in copies:
        copy.wait()


def per_device(seqs, heads, lin_qk, lin_v, conv_qk, conv_v, swa_qkv, head_gain):
    tokens = lin_qk.shape[0]
    width = lin_v.shape[1]
    local = width // DV
    chunks = tokens // C
    part = local * ROWS // seqs
    hbm = pl.BlockSpec(memory_space=pltpu.HBM)
    vmem = pl.BlockSpec(memory_space=pltpu.VMEM)
    dma = pltpu.SemaphoreType.DMA
    halos = 1 + 3 * local
    combined, squares = pl.pallas_call(
        functools.partial(kernel, seqs, heads),
        out_shape=(
            pltpu.VMEM((tokens, width), F32),
            pltpu.VMEM((chunks, 1, C), F32),
        ),
        in_specs=[hbm, hbm, hbm, vmem, vmem, vmem],
        out_specs=(vmem, vmem),
        scratch_shapes=[
            pltpu.VMEM((8 + tokens, 2 * DK * local), F32),
            pltpu.VMEM((local, 8 + tokens, DV), F32),
            pltpu.VMEM((local, tokens, DV), F32),
            pltpu.VMEM((2, local, WIN + tokens, DV), F32),
            pltpu.VMEM((tokens, 2 * DK * local), F32),
            pltpu.VMEM((chunks, 2 * local, 2 * DK, C), F32),
            pltpu.VMEM((local, tokens, 2 * DV), BF16),
            pltpu.VMEM((chunks + 1, local * ROWS, DV), F32),
            pltpu.VMEM((local, tokens, DV), F32),
            pltpu.VMEM((local, tokens, DV), F32),
            pltpu.VMEM((local * ROWS, DV), F32),
            pltpu.VMEM((seqs, part, DV), F32),
            pltpu.VMEM((seqs, part, DV), F32),
            pltpu.VMEM((local * ROWS, DV), F32),
            pltpu.VMEM((chunks, 1, C), F32),
            pltpu.VMEM((heads - 1, chunks, 1, C), F32),
            dma((QUARTERS, 1 + local)),
            dma((local, 3)),
            dma((halos,)),
            dma((halos,)),
            dma((seqs - 1,)),
            dma((seqs - 1,)),
            dma((seqs - 1,)),
            dma((seqs - 1,)),
            dma((heads - 1,)),
            dma((heads - 1,)),
        ],
        compiler_params=pltpu.CompilerParams(
            collective_id=0, has_side_effects=True, vmem_limit_bytes=54 * 1024 * 1024
        ),
        name="mixer",
    )(lin_qk, lin_v, jnp.transpose(swa_qkv, (1, 0, 2)), conv_qk, conv_v, head_gain[None])
    return pl.pallas_call(
        functools.partial(scale_kernel, heads * width),
        out_shape=jax.ShapeDtypeStruct((tokens, width), F32),
        in_specs=[vmem, vmem],
        out_specs=hbm,
        scratch_shapes=[pltpu.VMEM((tokens, width), F32), dma((chunks,))],
        compiler_params=pltpu.CompilerParams(vmem_limit_bytes=16 * 1024 * 1024),
        name="scale",
    )(combined, squares)


def solution(mesh):
    placed = (
        P("seq", "head"),
        P("seq", "head"),
        P(None, "head"),
        P(None, "head"),
        P("seq", None, "head"),
        P("head"),
    )
    return jax.shard_map(
        functools.partial(per_device, mesh.shape["seq"], mesh.shape["head"]),
        mesh=mesh, in_specs=placed, out_specs=P("seq", "head"), check_vma=False,
    )
```

```python
import functools
import math

import jax
import jax.numpy as jnp
from jax import lax
from jax.experimental import pallas as pl
from jax.experimental.pallas import tpu as pltpu
from jax.sharding import PartitionSpec as P

DK = 16
DV = 128
WIN = 64
C = 128
QUARTERS = 4
LOCAL_GROUP = 4
CARRIED_GROUP = 4
PREFIX_HEAD = 1
ROWS = 160
MESH = pl.DeviceIdType.MESH
F32 = jnp.float32
BF16 = jnp.bfloat16


def split(value):
    high = value.astype(BF16)
    low = (value - high.astype(F32)).astype(BF16)
    return high, low


def dot(left, right, dims=((1,), (0,))):
    return lax.dot_general(left, right, (dims, ((), ())), preferred_element_type=F32)


def fold(value):
    return value[:, :DV] + value[:, DV:]


def feature_rows(load, pair, linear, constant):
    base = load(0, DK)
    twice = base if pair == 1 else base * pair
    rows = [base * base]
    rows += [twice * load(shift, DK) for shift in range(1, DK // 2)]
    rows += [twice[: DK // 2] * load(DK // 2, DK // 2)]
    rows += [base if linear == 1 else base * linear]
    first = lax.broadcasted_iota(jnp.int32, (8, base.shape[1]), 0) == 0
    rows += [jnp.where(first, F32(constant), F32(0.0))]
    return jnp.concatenate(rows, axis=0)


def kernel(
    seqs, heads,
    qk_hbm, v_hbm, swa_hbm, wqk_ref, wv_ref, gain_ref,
    out_ref, total_ref,
    xin, vin, qin, kin, xs, xt, us, sx, lin, win,
    mine, got, prefs, pref, sq, sqgot,
    in_sem, swa_sem, hs_sem, hr_sem, s1, r1, s2, r2, s3, r3,
):
    tokens = xs.shape[0]
    local = vin.shape[0]
    chunks = tokens // C
    part = local * ROWS // seqs
    quarter = tokens // QUARTERS
    me = lax.axis_index("seq")
    my_head = lax.axis_index("head")

    def lin_loads(n):
        at = pl.multiple_of(n * quarter, 8)
        copies = [pltpu.make_async_copy(
            qk_hbm.at[pl.ds(at, quarter)], xin.at[pl.ds(8 + at, quarter)], in_sem.at[n, 0])]
        for h in range(local):
            copies.append(pltpu.make_async_copy(
                v_hbm.at[pl.ds(at, quarter), pl.ds(h * DV, DV)], vin.at[h, pl.ds(8 + at, quarter)],
                in_sem.at[n, 1 + h]))
        return copies

    for n in range(QUARTERS):
        for load in lin_loads(n):
            load.start()

    barrier = pltpu.get_barrier_semaphore()
    for step in range(1, seqs):
        pl.semaphore_signal(barrier, inc=1, device_id={"seq": lax.rem(me + step, seqs)}, device_id_type=MESH)
    for step in range(1, heads):
        pl.semaphore_signal(barrier, inc=1, device_id={"head": lax.rem(my_head + step, heads)}, device_id_type=MESH)

    def head_loads(h):
        columns = pl.ds(pl.multiple_of(h * DV, DV), DV)
        copies = [pltpu.make_async_copy(swa_hbm.at[0, :, columns], qin.at[h], swa_sem.at[h, 0])]
        for which in range(2):
            copies.append(pltpu.make_async_copy(
                swa_hbm.at[1 + which, :, columns], kin.at[which, h, pl.ds(WIN, tokens)], swa_sem.at[h, 1 + which]))
        return copies

    for h in range(local):
        for load in head_loads(h):
            load.start()
    after = {"seq": lax.rem(me + 1, seqs)}

    def remote(source, target, send, receive, device):
        return pltpu.make_async_remote_copy(
            src_ref=source, dst_ref=target, send_sem=send, recv_sem=receive, device_id=device, device_id_type=MESH)

    tail = pl.ds(tokens - 8, 8)
    halos = [remote(qk_hbm.at[tail], xin.at[pl.ds(0, 8)], hs_sem.at[0], hr_sem.at[0], after)]
    for h in range(local):
        halos.append(remote(v_hbm.at[tail, pl.ds(h * DV, DV)], vin.at[h, pl.ds(0, 8)],
                            hs_sem.at[1 + h], hr_sem.at[1 + h], after))
    window_halos = []
    for h in range(local):
        for which in range(2):
            slot = 1 + local + 2 * h + which
            window_halos.append(remote(
                swa_hbm.at[1 + which, pl.ds(tokens - WIN, WIN), pl.ds(h * DV, DV)],
                kin.at[which, h, pl.ds(0, WIN)], hs_sem.at[slot], hr_sem.at[slot], after))

    sx[0] = jnp.zeros(sx.shape[1:], F32)
    for load in lin_loads(0):
        load.wait()
    per_quarter = chunks // QUARTERS
    steps = chunks // 2

    def state_step(i, carry):
        last = i == steps - 1

        @pl.when((lax.rem(2 * i + 2, per_quarter) == 0) & jnp.logical_not(last))
        def _():
            for load in lin_loads((2 * i + 2) // per_quarter):
                load.wait()

        @pl.when(i == 1)
        def _():
            pl.semaphore_wait(barrier, seqs - 1 + heads - 1)
            for copy in halos + window_halos:
                copy.start()

        @pl.when(last)
        def _():
            for copy in halos:
                copy.wait_recv()
            keep = me > 0
            xin[pl.ds(0, 8)] = jnp.where(keep, xin[pl.ds(0, 8)], 0.0)
            for h in range(local):
                vin[h, pl.ds(0, 8)] = jnp.where(keep, vin[h, pl.ds(0, 8)], 0.0)

        which_chunks = (2 * i + 1, lax.rem(2 * i + 2, chunks))
        pairs = [(c, h) for c in range(2) for h in range(local)]
        turned = []
        for c in which_chunks:
            row = pl.multiple_of(c * C, C)
            x = wqk_ref[0:1] * xin[pl.ds(row + 6, C)]
            x = x + wqk_ref[1:2] * xin[pl.ds(row + 7, C)]
            x = x + wqk_ref[2:3] * xin[pl.ds(row + 8, C)]
            xs[pl.ds(row, C)] = x
            turned.append(x.T)
        boths = []
        for n, h in pairs:
            row = pl.multiple_of(which_chunks[n] * C, C)
            columns = slice(h * DV, (h + 1) * DV)
            u = wv_ref[0:1, columns] * vin[h, pl.ds(row + 6, C)]
            u = u + wv_ref[1:2, columns] * vin[h, pl.ds(row + 7, C)]
            u = u + wv_ref[2:3, columns] * vin[h, pl.ds(row + 8, C)]
            both = jnp.concatenate(split(u), axis=1)
            us[h, pl.ds(row, C)] = both
            boths.append(both)
        for c, value in zip(which_chunks, turned):
            for piece in range(2 * local):
                at = value[piece * DK:(piece + 1) * DK]
                xt[c, piece, 0:DK] = at
                xt[c, piece, DK:2 * DK] = at
        phis = []
        for n, h in pairs:
            c = which_chunks[n]
            phi = feature_rows(lambda start, size: xt[c, 2 * h + 1, start:start + size], 1, 1, 1.0)
            phis.append(jnp.concatenate(split(phi), axis=1))
        states = [dot(phi, jnp.concatenate([both, both], axis=0)) for phi, both in zip(phis, boths)]
        again = jnp.where(last, 0.0, 1.0).astype(F32)
        for h in range(local):
            rows = slice(h * ROWS, (h + 1) * ROWS)
            total = sx[2 * i, rows] + fold(states[h])
            sx[2 * i + 1, rows] = total
            sx[2 * i + 2, rows] = total * again + fold(states[local + h])
        return carry

    lax.fori_loop(0, steps, state_step, 0)

    mine[...] = sx[chunks - 1] + sx[chunks]
    first = []
    for step in range(1, seqs):
        peer = lax.rem(me + step, seqs)
        rows = pl.ds(pl.multiple_of(peer * part, 8), part)
        first.append(remote(mine.at[rows], got.at[me], s1.at[step - 1], r1.at[step - 1], {"seq": peer}))
        first[-1].start()
    got[me] = mine[pl.ds(pl.multiple_of(me * part, 8), part)]

    lane = lax.broadcasted_iota(jnp.int32, (C, C), 1)
    sub = lax.broadcasted_iota(jnp.int32, (C, C), 0)
    query_lane = lax.rem(lane, 2 * DK) < DK
    causal = lane <= sub

    def local_step(i, carry):
        which_chunks = [LOCAL_GROUP * i + n for n in range(LOCAL_GROUP)]
        at_rows = [pl.ds(pl.multiple_of(c * C, C), C) for c in which_chunks]
        lefts = []
        for rows in at_rows:
            x = xs[rows]
            lefts.append(jnp.concatenate(split(jnp.where(query_lane, x, pltpu.roll(x, DK, 1))), axis=1))
        rights = []
        for c in which_chunks:
            for pair in range(local // 2):
                sides = []
                for h in (2 * pair, 2 * pair + 1):
                    high, low = split(xt[c, 2 * h + 1, 0:DK])
                    blank = jnp.zeros((DK, C), BF16)
                    pieces = [blank] * (2 * 2 * local)
                    pieces[2 * h] = high
                    pieces[2 * h + 1] = low
                    pieces[2 * local + 2 * h] = high
                    sides.append(jnp.concatenate(pieces, axis=0))
                rights.append(jnp.concatenate(sides, axis=1))
        scores = [dot(lefts[n], rights[n * (local // 2) + pair])
                  for n in range(LOCAL_GROUP) for pair in range(local // 2)]
        values = []
        for score in scores:
            for which in range(2):
                value = score[:, which * C:(which + 1) * C] + 4.0
                value = jnp.where(causal, value * value + 16.0, 0.0)
                values.append(jnp.concatenate(split(value), axis=1))
        sums = []
        for n in range(LOCAL_GROUP):
            for h in range(local):
                both = us[h, at_rows[n]]
                sums.append(dot(values[n * local + h], jnp.concatenate([both, both], axis=0)))
        for n in range(LOCAL_GROUP):
            for h in range(local):
                lin[h, at_rows[n]] = fold(sums[n * local + h])
        return carry

    lax.fori_loop(0, chunks // LOCAL_GROUP, local_step, 0)

    own_rows = pl.ds(pl.multiple_of(me * part, 8), part)
    second = []
    for step in range(1, seqs):
        peer = lax.rem(me + step, seqs)
        second.append(remote(prefs.at[peer], pref.at[own_rows], s2.at[step - 1], r2.at[step - 1], {"seq": peer}))

    def prefix_step(d, carry):
        prefs[d] = carry
        return carry + got[d]

    key = lax.broadcasted_iota(jnp.int32, (WIN, C), 1)
    query = lax.broadcasted_iota(jnp.int32, (WIN, C), 0)
    scale = math.log2(math.e) / math.sqrt(DV)
    own_half = lax.rem(lax.broadcasted_iota(jnp.int32, (C, 2 * C), 1), C) < WIN
    inside = ((key < WIN) & (key <= query)) | ((key >= WIN) & (key - C > query - WIN))
    lowest = jnp.where(me == 0, C, 0)
    starts = inside & ((key < WIN) | (key >= lowest))
    bias_first = jnp.where(starts, 0.0, -1e30).astype(F32)
    bias_even = jnp.where(inside, 0.0, -1e30).astype(F32)
    bias_odd = jnp.where((key <= query + WIN) & (key > query), 0.0, -1e30).astype(F32)

    def split_queries(value):
        return jnp.concatenate(split(value * scale), axis=1)

    def split_values(h, j):
        return jnp.concatenate(split(kin[1, h, pl.ds(j * WIN, WIN)]), axis=1)

    def softmax(score):
        weight = jnp.exp2(score - jnp.max(score, axis=1, keepdims=True))
        return jnp.concatenate(split(weight), axis=1), jnp.sum(weight, axis=1, keepdims=True)

    def window_step(h, carry):
        @pl.when(h == PREFIX_HEAD)
        def _():
            for copy in first:
                copy.wait_recv()
            lax.fori_loop(0, seqs, prefix_step, jnp.zeros((part, DV), F32))
            for copy in second:
                copy.start()
            pref[own_rows] = prefs[me]

        for load in head_loads(h):
            load.wait()
        tiles = [jnp.concatenate(split(kin[0, h, pl.ds(WIN + j * C, C)].T), axis=1) for j in range(chunks)]
        scores = []
        for j in range(chunks):
            own = tiles[j]
            q_both = split_queries(qin[h, pl.ds(j * C, C)])
            if j > 0:
                ring = jnp.where(own_half, own, tiles[j - 1])
                scores.append(fold(dot(q_both[:WIN], jnp.concatenate([ring, ring], axis=0))) + bias_even)
            scores.append(fold(dot(q_both[WIN:], jnp.concatenate([own, own], axis=0))) + bias_odd)
        weights = [softmax(score) for score in scores]
        values = [split_values(h, j) for j in range(1, 2 * chunks + 1)]
        for j, (weight, norm) in enumerate(weights, 1):
            even = j if j % 2 else j + 1
            odd = j + 1 if j % 2 else j
            tile = [values[even - 1], values[odd - 1]]
            win[h, pl.ds(j * WIN, WIN)] = fold(dot(weight, jnp.concatenate(tile + tile, axis=0))) / norm
        return carry

    lax.fori_loop(0, local, window_step, 0)

    for copy in window_halos:
        copy.wait_recv()
    rings = [jnp.concatenate(split(jnp.concatenate(
        [kin[0, h, pl.ds(WIN, WIN)], kin[0, h, pl.ds(0, WIN)]], axis=0).T), axis=1) for h in range(local)]
    openings = [fold(dot(split_queries(qin[h, pl.ds(0, WIN)]), jnp.concatenate([ring, ring], axis=0))) + bias_first
                for h, ring in enumerate(rings)]
    for h, (weight, norm) in enumerate([softmax(score) for score in openings]):
        tile = [split_values(h, 1), split_values(h, 0)]
        win[h, pl.ds(0, WIN)] = fold(dot(weight, jnp.concatenate(tile + tile, axis=0))) / norm

    for copy in second:
        copy.wait_recv()

    def carried_step(i, carry):
        which_chunks = [CARRIED_GROUP * i + n for n in range(CARRIED_GROUP)]
        at_rows = [pl.ds(pl.multiple_of(c * C, C), C) for c in which_chunks]
        pairs = [(n, h) for n in range(CARRIED_GROUP) for h in range(local)]
        phis = []
        for n, h in pairs:
            phi = feature_rows(
                lambda start, size: xt[which_chunks[n], 2 * h, start:start + size], 2.0, 8.0, 32.0)
            phis.append(jnp.concatenate(split(phi), axis=0).T)
        states = []
        for n, h in pairs:
            c = which_chunks[n]
            rows = slice(h * ROWS, (h + 1) * ROWS)
            later = jnp.where(c > 0, 1.0, 0.0).astype(F32)
            state = sx[jnp.maximum(c - 1, 0), rows] + (pref[rows] + sx[chunks, rows] * later)
            both = jnp.concatenate(split(state), axis=1)
            states.append(jnp.concatenate([both, both], axis=0))
        earlier = [dot(phi, state) for phi, state in zip(phis, states)]
        mixes = [lin[h, at_rows[n]] + fold(earlier[n * local + h]) for n, h in pairs]
        means = [jnp.sum(mix * mix, axis=1, keepdims=True) * (1.0 / DV) for mix in mixes]
        squares = [jnp.zeros((C, DV), F32) for _ in which_chunks]
        for (n, h), mix, mean in zip(pairs, mixes, means):
            columns = slice(h * DV, (h + 1) * DV)
            value = mix * lax.rsqrt(mean + 1024.0e-6) * gain_ref[0:1, columns] + win[h, at_rows[n]]
            out_ref[at_rows[n], columns] = value
            squares[n] = squares[n] + value * value
        for c, square in zip(which_chunks, squares):
            sq[c] = jnp.sum(square.T, axis=0, keepdims=True)
        return carry

    lax.fori_loop(0, chunks // CARRIED_GROUP, carried_step, 0)

    third = []
    for step in range(1, heads):
        peer = lax.rem(my_head + step, heads)
        third.append(remote(sq, sqgot.at[step - 1], s3.at[step - 1], r3.at[step - 1], {"head": peer}))
        third[-1].start()
    for copy in halos + window_halos + first + second:
        copy.wait_send()
    total = sq[...]
    for step, copy in enumerate(third):
        copy.wait_recv()
        total = total + sqgot[step]
    total_ref[...] = total
    for copy in third:
        copy.wait_send()


def scale_kernel(count, value_ref, total_ref, out_hbm, stage, sems):
    chunks, width = total_ref.shape[0], value_ref.shape[1]
    copies = []
    for c in range(chunks):
        rows = pl.ds(c * C, C)
        factor = lax.rsqrt(total_ref[c] * (1.0 / count) + 1e-06)
        factor = jnp.broadcast_to(factor, (C, C)).T
        for h in range(width // DV):
            columns = slice(h * DV, (h + 1) * DV)
            stage[rows, columns] = value_ref[rows, columns] * factor
        copies.append(pltpu.make_async_copy(stage.at[rows], out_hbm.at[rows], sems.at[c]))
        copies[-1].start()
    for copy in copies:
        copy.wait()


def per_device(seqs, heads, lin_qk, lin_v, conv_qk, conv_v, swa_qkv, head_gain):
    tokens = lin_qk.shape[0]
    width = lin_v.shape[1]
    local = width // DV
    chunks = tokens // C
    part = local * ROWS // seqs
    hbm = pl.BlockSpec(memory_space=pltpu.HBM)
    vmem = pl.BlockSpec(memory_space=pltpu.VMEM)
    dma = pltpu.SemaphoreType.DMA
    halos = 1 + 3 * local
    combined, squares = pl.pallas_call(
        functools.partial(kernel, seqs, heads),
        out_shape=(
            pltpu.VMEM((tokens, width), F32),
            pltpu.VMEM((chunks, 1, C), F32),
        ),
        in_specs=[hbm, hbm, hbm, vmem, vmem, vmem],
        out_specs=(vmem, vmem),
        scratch_shapes=[
            pltpu.VMEM((8 + tokens, 2 * DK * local), F32),
            pltpu.VMEM((local, 8 + tokens, DV), F32),
            pltpu.VMEM((local, tokens, DV), F32),
            pltpu.VMEM((2, local, WIN + tokens, DV), F32),
            pltpu.VMEM((tokens, 2 * DK * local), F32),
            pltpu.VMEM((chunks, 2 * local, 2 * DK, C), F32),
            pltpu.VMEM((local, tokens, 2 * DV), BF16),
            pltpu.VMEM((chunks + 1, local * ROWS, DV), F32),
            pltpu.VMEM((local, tokens, DV), F32),
            pltpu.VMEM((local, tokens, DV), F32),
            pltpu.VMEM((local * ROWS, DV), F32),
            pltpu.VMEM((seqs, part, DV), F32),
            pltpu.VMEM((seqs, part, DV), F32),
            pltpu.VMEM((local * ROWS, DV), F32),
            pltpu.VMEM((chunks, 1, C), F32),
            pltpu.VMEM((heads - 1, chunks, 1, C), F32),
            dma((QUARTERS, 1 + local)),
            dma((local, 3)),
            dma((halos,)),
            dma((halos,)),
            dma((seqs - 1,)),
            dma((seqs - 1,)),
            dma((seqs - 1,)),
            dma((seqs - 1,)),
            dma((heads - 1,)),
            dma((heads - 1,)),
        ],
        compiler_params=pltpu.CompilerParams(
            collective_id=0, has_side_effects=True, vmem_limit_bytes=54 * 1024 * 1024
        ),
        name="mixer",
    )(lin_qk, lin_v, jnp.transpose(swa_qkv, (1, 0, 2)), conv_qk, conv_v, head_gain[None])
    return pl.pallas_call(
        functools.partial(scale_kernel, heads * width),
        out_shape=jax.ShapeDtypeStruct((tokens, width), F32),
        in_specs=[vmem, vmem],
        out_specs=hbm,
        scratch_shapes=[pltpu.VMEM((tokens, width), F32), dma((chunks,))],
        compiler_params=pltpu.CompilerParams(vmem_limit_bytes=16 * 1024 * 1024),
        name="scale",
    )(combined, squares)


def solution(mesh):
    placed = (
        P("seq", "head"),
        P("seq", "head"),
        P(None, "head"),
        P(None, "head"),
        P("seq", None, "head"),
        P("head"),
    )
    return jax.shard_map(
        functools.partial(per_device, mesh.shape["seq"], mesh.shape["head"]),
        mesh=mesh, in_specs=placed, out_specs=P("seq", "head"), check_vma=False,
    )
```

```python
import functools
import math

import jax
import jax.numpy as jnp
from jax import lax
from jax.experimental import pallas as pl
from jax.experimental.pallas import tpu as pltpu
from jax.sharding import PartitionSpec as P

DK = 16
DV = 128
WIN = 64
C = 128
QUARTERS = 4
LOCAL_GROUP = 4
CARRIED_GROUP = 4
PREFIX_HEAD = 0
ROWS = 160
MESH = pl.DeviceIdType.MESH
F32 = jnp.float32
BF16 = jnp.bfloat16


def split(value):
    high = value.astype(BF16)
    low = (value - high.astype(F32)).astype(BF16)
    return high, low


def dot(left, right, dims=((1,), (0,))):
    return lax.dot_general(left, right, (dims, ((), ())), preferred_element_type=F32)


def fold(value):
    return value[:, :DV] + value[:, DV:]


def feature_rows(load, pair, linear, constant):
    base = load(0, DK)
    twice = base if pair == 1 else base * pair
    rows = [base * base]
    rows += [twice * load(shift, DK) for shift in range(1, DK // 2)]
    rows += [twice[: DK // 2] * load(DK // 2, DK // 2)]
    rows += [base if linear == 1 else base * linear]
    first = lax.broadcasted_iota(jnp.int32, (8, base.shape[1]), 0) == 0
    rows += [jnp.where(first, F32(constant), F32(0.0))]
    return jnp.concatenate(rows, axis=0)


def kernel(
    seqs, heads,
    qk_hbm, v_hbm, swa_hbm, wqk_ref, wv_ref, gain_ref,
    out_ref, total_ref,
    xin, vin, qin, kin, xs, xt, us, sx, lin, win,
    mine, got, prefs, pref, sq, sqgot,
    in_sem, swa_sem, hs_sem, hr_sem, s1, r1, s2, r2, s3, r3,
):
    tokens = xs.shape[0]
    local = vin.shape[0]
    chunks = tokens // C
    part = local * ROWS // seqs
    quarter = tokens // QUARTERS
    me = lax.axis_index("seq")
    my_head = lax.axis_index("head")

    def lin_loads(n):
        at = pl.multiple_of(n * quarter, 8)
        copies = [pltpu.make_async_copy(
            qk_hbm.at[pl.ds(at, quarter)], xin.at[pl.ds(8 + at, quarter)], in_sem.at[n, 0])]
        for h in range(local):
            copies.append(pltpu.make_async_copy(
                v_hbm.at[pl.ds(at, quarter), pl.ds(h * DV, DV)], vin.at[h, pl.ds(8 + at, quarter)],
                in_sem.at[n, 1 + h]))
        return copies

    for n in range(QUARTERS):
        for load in lin_loads(n):
            load.start()

    barrier = pltpu.get_barrier_semaphore()
    for step in range(1, seqs):
        pl.semaphore_signal(barrier, inc=1, device_id={"seq": lax.rem(me + step, seqs)}, device_id_type=MESH)
    for step in range(1, heads):
        pl.semaphore_signal(barrier, inc=1, device_id={"head": lax.rem(my_head + step, heads)}, device_id_type=MESH)

    def head_loads(h):
        columns = pl.ds(pl.multiple_of(h * DV, DV), DV)
        copies = [pltpu.make_async_copy(swa_hbm.at[0, :, columns], qin.at[h], swa_sem.at[h, 0])]
        for which in range(2):
            copies.append(pltpu.make_async_copy(
                swa_hbm.at[1 + which, :, columns], kin.at[which, h, pl.ds(WIN, tokens)], swa_sem.at[h, 1 + which]))
        return copies

    for h in range(local):
        for load in head_loads(h):
            load.start()
    after = {"seq": lax.rem(me + 1, seqs)}

    def remote(source, target, send, receive, device):
        return pltpu.make_async_remote_copy(
            src_ref=source, dst_ref=target, send_sem=send, recv_sem=receive, device_id=device, device_id_type=MESH)

    tail = pl.ds(tokens - 8, 8)
    halos = [remote(qk_hbm.at[tail], xin.at[pl.ds(0, 8)], hs_sem.at[0], hr_sem.at[0], after)]
    for h in range(local):
        halos.append(remote(v_hbm.at[tail, pl.ds(h * DV, DV)], vin.at[h, pl.ds(0, 8)],
                            hs_sem.at[1 + h], hr_sem.at[1 + h], after))
    window_halos = []
    for h in range(local):
        for which in range(2):
            slot = 1 + local + 2 * h + which
            window_halos.append(remote(
                swa_hbm.at[1 + which, pl.ds(tokens - WIN, WIN), pl.ds(h * DV, DV)],
                kin.at[which, h, pl.ds(0, WIN)], hs_sem.at[slot], hr_sem.at[slot], after))

    pl.semaphore_wait(barrier, seqs - 1 + heads - 1)
    for copy in halos + window_halos[::2]:
        copy.start()
    sx[0] = jnp.zeros(sx.shape[1:], F32)
    for load in lin_loads(0):
        load.wait()
    per_quarter = chunks // QUARTERS
    steps = chunks // 2

    def state_step(i, carry):
        last = i == steps - 1

        @pl.when((lax.rem(2 * i + 2, per_quarter) == 0) & jnp.logical_not(last))
        def _():
            for load in lin_loads((2 * i + 2) // per_quarter):
                load.wait()

        @pl.when(last)
        def _():
            for copy in halos:
                copy.wait_recv()
            keep = me > 0
            xin[pl.ds(0, 8)] = jnp.where(keep, xin[pl.ds(0, 8)], 0.0)
            for h in range(local):
                vin[h, pl.ds(0, 8)] = jnp.where(keep, vin[h, pl.ds(0, 8)], 0.0)

        which_chunks = (2 * i + 1, lax.rem(2 * i + 2, chunks))
        pairs = [(c, h) for c in range(2) for h in range(local)]
        turned = []
        for c in which_chunks:
            row = pl.multiple_of(c * C, C)
            x = wqk_ref[0:1] * xin[pl.ds(row + 6, C)]
            x = x + wqk_ref[1:2] * xin[pl.ds(row + 7, C)]
            x = x + wqk_ref[2:3] * xin[pl.ds(row + 8, C)]
            xs[pl.ds(row, C)] = x
            turned.append(x.T)
        boths = []
        for n, h in pairs:
            row = pl.multiple_of(which_chunks[n] * C, C)
            columns = slice(h * DV, (h + 1) * DV)
            u = wv_ref[0:1, columns] * vin[h, pl.ds(row + 6, C)]
            u = u + wv_ref[1:2, columns] * vin[h, pl.ds(row + 7, C)]
            u = u + wv_ref[2:3, columns] * vin[h, pl.ds(row + 8, C)]
            both = jnp.concatenate(split(u), axis=1)
            us[h, pl.ds(row, C)] = both
            boths.append(both)
        for c, value in zip(which_chunks, turned):
            for piece in range(2 * local):
                at = value[piece * DK:(piece + 1) * DK]
                xt[c, piece, 0:DK] = at
                xt[c, piece, DK:2 * DK] = at
        phis = []
        for n, h in pairs:
            c = which_chunks[n]
            phi = feature_rows(lambda start, size: xt[c, 2 * h + 1, start:start + size], 1, 1, 1.0)
            phis.append(jnp.concatenate(split(phi), axis=1))
        states = [dot(phi, jnp.concatenate([both, both], axis=0)) for phi, both in zip(phis, boths)]
        again = jnp.where(last, 0.0, 1.0).astype(F32)
        for h in range(local):
            rows = slice(h * ROWS, (h + 1) * ROWS)
            total = sx[2 * i, rows] + fold(states[h])
            sx[2 * i + 1, rows] = total
            sx[2 * i + 2, rows] = total * again + fold(states[local + h])
        return carry

    lax.fori_loop(0, steps, state_step, 0)

    mine[...] = sx[chunks - 1] + sx[chunks]
    first = []
    for step in range(1, seqs):
        peer = lax.rem(me + step, seqs)
        rows = pl.ds(pl.multiple_of(peer * part, 8), part)
        first.append(remote(mine.at[rows], got.at[me], s1.at[step - 1], r1.at[step - 1], {"seq": peer}))
        first[-1].start()
    got[me] = mine[pl.ds(pl.multiple_of(me * part, 8), part)]

    lane = lax.broadcasted_iota(jnp.int32, (C, C), 1)
    sub = lax.broadcasted_iota(jnp.int32, (C, C), 0)
    query_lane = lax.rem(lane, 2 * DK) < DK
    causal = lane <= sub

    def local_step(i, carry):
        which_chunks = [LOCAL_GROUP * i + n for n in range(LOCAL_GROUP)]
        at_rows = [pl.ds(pl.multiple_of(c * C, C), C) for c in which_chunks]
        lefts = []
        for rows in at_rows:
            x = xs[rows]
            lefts.append(jnp.concatenate(split(jnp.where(query_lane, x, pltpu.roll(x, DK, 1))), axis=1))
        rights = []
        for c in which_chunks:
            for pair in range(local // 2):
                sides = []
                for h in (2 * pair, 2 * pair + 1):
                    high, low = split(xt[c, 2 * h + 1, 0:DK])
                    blank = jnp.zeros((DK, C), BF16)
                    pieces = [blank] * (2 * 2 * local)
                    pieces[2 * h] = high
                    pieces[2 * h + 1] = low
                    pieces[2 * local + 2 * h] = high
                    sides.append(jnp.concatenate(pieces, axis=0))
                rights.append(jnp.concatenate(sides, axis=1))
        scores = [dot(lefts[n], rights[n * (local // 2) + pair])
                  for n in range(LOCAL_GROUP) for pair in range(local // 2)]
        values = []
        for score in scores:
            for which in range(2):
                value = score[:, which * C:(which + 1) * C] + 4.0
                value = jnp.where(causal, value * value + 16.0, 0.0)
                values.append(jnp.concatenate(split(value), axis=1))
        sums = []
        for n in range(LOCAL_GROUP):
            for h in range(local):
                both = us[h, at_rows[n]]
                sums.append(dot(values[n * local + h], jnp.concatenate([both, both], axis=0)))
        for n in range(LOCAL_GROUP):
            for h in range(local):
                lin[h, at_rows[n]] = fold(sums[n * local + h])
        return carry

    lax.fori_loop(0, chunks // LOCAL_GROUP, local_step, 0)

    own_rows = pl.ds(pl.multiple_of(me * part, 8), part)
    second = []
    for step in range(1, seqs):
        peer = lax.rem(me + step, seqs)
        second.append(remote(prefs.at[peer], pref.at[own_rows], s2.at[step - 1], r2.at[step - 1], {"seq": peer}))

    def prefix_step(d, carry):
        prefs[d] = carry
        return carry + got[d]

    key = lax.broadcasted_iota(jnp.int32, (WIN, C), 1)
    query = lax.broadcasted_iota(jnp.int32, (WIN, C), 0)
    scale = math.log2(math.e) / math.sqrt(DV)
    own_half = lax.rem(lax.broadcasted_iota(jnp.int32, (C, 2 * C), 1), C) < WIN
    inside = ((key < WIN) & (key <= query)) | ((key >= WIN) & (key - C > query - WIN))
    lowest = jnp.where(me == 0, C, 0)
    starts = inside & ((key < WIN) | (key >= lowest))
    bias_first = jnp.where(starts, 0.0, -1e30).astype(F32)
    bias_even = jnp.where(inside, 0.0, -1e30).astype(F32)
    bias_odd = jnp.where((key <= query + WIN) & (key > query), 0.0, -1e30).astype(F32)

    def split_queries(value):
        return jnp.concatenate(split(value * scale), axis=1)

    def split_values(h, j):
        return jnp.concatenate(split(kin[1, h, pl.ds(j * WIN, WIN)]), axis=1)

    def softmax(score):
        weight = jnp.exp2(score - jnp.max(score, axis=1, keepdims=True))
        return jnp.concatenate(split(weight), axis=1), jnp.sum(weight, axis=1, keepdims=True)

    def window_step(h, carry):
        @pl.when(h == PREFIX_HEAD)
        def _():
            for copy in first:
                copy.wait_recv()
            lax.fori_loop(0, seqs, prefix_step, jnp.zeros((part, DV), F32))
            for copy in second:
                copy.start()
            pref[own_rows] = prefs[me]
            for copy in window_halos[1::2]:
                copy.start()

        for load in head_loads(h):
            load.wait()
        tiles = [jnp.concatenate(split(kin[0, h, pl.ds(WIN + j * C, C)].T), axis=1) for j in range(chunks)]
        scores = []
        for j in range(chunks):
            own = tiles[j]
            q_both = split_queries(qin[h, pl.ds(j * C, C)])
            if j > 0:
                ring = jnp.where(own_half, own, tiles[j - 1])
                scores.append(fold(dot(q_both[:WIN], jnp.concatenate([ring, ring], axis=0))) + bias_even)
            scores.append(fold(dot(q_both[WIN:], jnp.concatenate([own, own], axis=0))) + bias_odd)
        weights = [softmax(score) for score in scores]
        values = [split_values(h, j) for j in range(1, 2 * chunks + 1)]
        for j, (weight, norm) in enumerate(weights, 1):
            even = j if j % 2 else j + 1
            odd = j + 1 if j % 2 else j
            tile = [values[even - 1], values[odd - 1]]
            win[h, pl.ds(j * WIN, WIN)] = fold(dot(weight, jnp.concatenate(tile + tile, axis=0))) / norm
        return carry

    lax.fori_loop(0, local, window_step, 0)

    def opening_step():
        for copy in window_halos:
            copy.wait_recv()
        rings = [jnp.concatenate(split(jnp.concatenate(
            [kin[0, h, pl.ds(WIN, WIN)], kin[0, h, pl.ds(0, WIN)]], axis=0).T), axis=1) for h in range(local)]
        openings = [fold(dot(split_queries(qin[h, pl.ds(0, WIN)]), jnp.concatenate([ring, ring], axis=0))) + bias_first
                    for h, ring in enumerate(rings)]
        for h, (weight, norm) in enumerate([softmax(score) for score in openings]):
            tile = [split_values(h, 1), split_values(h, 0)]
            win[h, pl.ds(0, WIN)] = fold(dot(weight, jnp.concatenate(tile + tile, axis=0))) / norm

    for copy in second:
        copy.wait_recv()

    def carried_step(i, carry):
        group = chunks // CARRIED_GROUP - 1 - i
        which_chunks = [CARRIED_GROUP * group + n for n in range(CARRIED_GROUP)]

        @pl.when(group == 0)
        def _():
            opening_step()

        at_rows = [pl.ds(pl.multiple_of(c * C, C), C) for c in which_chunks]
        pairs = [(n, h) for n in range(CARRIED_GROUP) for h in range(local)]
        phis = []
        for n, h in pairs:
            phi = feature_rows(
                lambda start, size: xt[which_chunks[n], 2 * h, start:start + size], 2.0, 8.0, 32.0)
            phis.append(jnp.concatenate(split(phi), axis=0).T)
        states = []
        for n, h in pairs:
            c = which_chunks[n]
            rows = slice(h * ROWS, (h + 1) * ROWS)
            later = jnp.where(c > 0, 1.0, 0.0).astype(F32)
            state = sx[jnp.maximum(c - 1, 0), rows] + (pref[rows] + sx[chunks, rows] * later)
            both = jnp.concatenate(split(state), axis=1)
            states.append(jnp.concatenate([both, both], axis=0))
        earlier = [dot(phi, state) for phi, state in zip(phis, states)]
        mixes = [lin[h, at_rows[n]] + fold(earlier[n * local + h]) for n, h in pairs]
        means = [jnp.sum(mix * mix, axis=1, keepdims=True) * (1.0 / DV) for mix in mixes]
        squares = [jnp.zeros((C, DV), F32) for _ in which_chunks]
        for (n, h), mix, mean in zip(pairs, mixes, means):
            columns = slice(h * DV, (h + 1) * DV)
            value = mix * lax.rsqrt(mean + 1024.0e-6) * gain_ref[0:1, columns] + win[h, at_rows[n]]
            out_ref[at_rows[n], columns] = value
            squares[n] = squares[n] + value * value
        for c, square in zip(which_chunks, squares):
            sq[c] = jnp.sum(square.T, axis=0, keepdims=True)
        return carry

    lax.fori_loop(0, chunks // CARRIED_GROUP, carried_step, 0)

    third = []
    for step in range(1, heads):
        peer = lax.rem(my_head + step, heads)
        third.append(remote(sq, sqgot.at[step - 1], s3.at[step - 1], r3.at[step - 1], {"head": peer}))
        third[-1].start()
    for copy in halos + window_halos + first + second:
        copy.wait_send()
    total = sq[...]
    for step, copy in enumerate(third):
        copy.wait_recv()
        total = total + sqgot[step]
    total_ref[...] = total
    for copy in third:
        copy.wait_send()


def scale_kernel(count, value_ref, total_ref, out_hbm, stage, sems):
    chunks, width = total_ref.shape[0], value_ref.shape[1]
    copies = []
    for c in range(chunks):
        rows = pl.ds(c * C, C)
        factor = lax.rsqrt(total_ref[c] * (1.0 / count) + 1e-06)
        factor = jnp.broadcast_to(factor, (C, C)).T
        for h in range(width // DV):
            columns = slice(h * DV, (h + 1) * DV)
            stage[rows, columns] = value_ref[rows, columns] * factor
        copies.append(pltpu.make_async_copy(stage.at[rows], out_hbm.at[rows], sems.at[c]))
        copies[-1].start()
    for copy in copies:
        copy.wait()


def per_device(seqs, heads, lin_qk, lin_v, conv_qk, conv_v, swa_qkv, head_gain):
    tokens = lin_qk.shape[0]
    width = lin_v.shape[1]
    local = width // DV
    chunks = tokens // C
    part = local * ROWS // seqs
    hbm = pl.BlockSpec(memory_space=pltpu.HBM)
    vmem = pl.BlockSpec(memory_space=pltpu.VMEM)
    dma = pltpu.SemaphoreType.DMA
    halos = 1 + 3 * local
    combined, squares = pl.pallas_call(
        functools.partial(kernel, seqs, heads),
        out_shape=(
            pltpu.VMEM((tokens, width), F32),
            pltpu.VMEM((chunks, 1, C), F32),
        ),
        in_specs=[hbm, hbm, hbm, vmem, vmem, vmem],
        out_specs=(vmem, vmem),
        scratch_shapes=[
            pltpu.VMEM((8 + tokens, 2 * DK * local), F32),
            pltpu.VMEM((local, 8 + tokens, DV), F32),
            pltpu.VMEM((local, tokens, DV), F32),
            pltpu.VMEM((2, local, WIN + tokens, DV), F32),
            pltpu.VMEM((tokens, 2 * DK * local), F32),
            pltpu.VMEM((chunks, 2 * local, 2 * DK, C), F32),
            pltpu.VMEM((local, tokens, 2 * DV), BF16),
            pltpu.VMEM((chunks + 1, local * ROWS, DV), F32),
            pltpu.VMEM((local, tokens, DV), F32),
            pltpu.VMEM((local, tokens, DV), F32),
            pltpu.VMEM((local * ROWS, DV), F32),
            pltpu.VMEM((seqs, part, DV), F32),
            pltpu.VMEM((seqs, part, DV), F32),
            pltpu.VMEM((local * ROWS, DV), F32),
            pltpu.VMEM((chunks, 1, C), F32),
            pltpu.VMEM((heads - 1, chunks, 1, C), F32),
            dma((QUARTERS, 1 + local)),
            dma((local, 3)),
            dma((halos,)),
            dma((halos,)),
            dma((seqs - 1,)),
            dma((seqs - 1,)),
            dma((seqs - 1,)),
            dma((seqs - 1,)),
            dma((heads - 1,)),
            dma((heads - 1,)),
        ],
        compiler_params=pltpu.CompilerParams(
            collective_id=0, has_side_effects=True, vmem_limit_bytes=54 * 1024 * 1024
        ),
        name="mixer",
    )(lin_qk, lin_v, jnp.transpose(swa_qkv, (1, 0, 2)), conv_qk, conv_v, head_gain[None])
    return pl.pallas_call(
        functools.partial(scale_kernel, heads * width),
        out_shape=jax.ShapeDtypeStruct((tokens, width), F32),
        in_specs=[vmem, vmem],
        out_specs=hbm,
        scratch_shapes=[pltpu.VMEM((tokens, width), F32), dma((chunks,))],
        compiler_params=pltpu.CompilerParams(vmem_limit_bytes=16 * 1024 * 1024),
        name="scale",
    )(combined, squares)


def solution(mesh):
    placed = (
        P("seq", "head"),
        P("seq", "head"),
        P(None, "head"),
        P(None, "head"),
        P("seq", None, "head"),
        P("head"),
    )
    return jax.shard_map(
        functools.partial(per_device, mesh.shape["seq"], mesh.shape["head"]),
        mesh=mesh, in_specs=placed, out_specs=P("seq", "head"), check_vma=False,
    )
```

```python
import functools
import math

import jax
import jax.numpy as jnp
from jax import lax
from jax.experimental import pallas as pl
from jax.experimental.pallas import tpu as pltpu
from jax.sharding import PartitionSpec as P

DK = 16
DV = 128
WIN = 64
C = 128
QUARTERS = 4
LOCAL_GROUP = 4
CARRIED_GROUP = 4
PREFIX_HEAD = 0
ROWS = 160
MESH = pl.DeviceIdType.MESH
F32 = jnp.float32
BF16 = jnp.bfloat16


def split(value):
    high = value.astype(BF16)
    low = (value - high.astype(F32)).astype(BF16)
    return high, low


def dot(left, right, dims=((1,), (0,))):
    return lax.dot_general(left, right, (dims, ((), ())), preferred_element_type=F32)


def fold(value):
    return value[:, :DV] + value[:, DV:]


def feature_rows(load, pair, linear, constant):
    base = load(0, DK)
    twice = base if pair == 1 else base * pair
    rows = [base * base]
    rows += [twice * load(shift, DK) for shift in range(1, DK // 2)]
    rows += [twice[: DK // 2] * load(DK // 2, DK // 2)]
    rows += [base if linear == 1 else base * linear]
    first = lax.broadcasted_iota(jnp.int32, (8, base.shape[1]), 0) == 0
    rows += [jnp.where(first, F32(constant), F32(0.0))]
    return jnp.concatenate(rows, axis=0)


def far_first(seqs):
    side = math.isqrt(seqs)
    return sorted(range(1, seqs), key=lambda step: -sum(
        min(at, side - at) for at in (step // side, step % side)))


def kernel(
    seqs, heads,
    qk_hbm, v_hbm, swa_hbm, wqk_ref, wv_ref, gain_ref,
    out_ref, total_ref,
    xin, vin, qin, kin, xs, xt, us, sx, lin, win,
    mine, got, prefs, pref, sq, sqgot,
    in_sem, swa_sem, hs_sem, hr_sem, s1, r1, s2, r2, s3, r3,
):
    tokens = xs.shape[0]
    local = vin.shape[0]
    chunks = tokens // C
    part = local * ROWS // seqs
    quarter = tokens // QUARTERS
    me = lax.axis_index("seq")
    my_head = lax.axis_index("head")

    def lin_loads(n):
        at = pl.multiple_of(n * quarter, 8)
        copies = [pltpu.make_async_copy(
            qk_hbm.at[pl.ds(at, quarter)], xin.at[pl.ds(8 + at, quarter)], in_sem.at[n, 0])]
        for h in range(local):
            copies.append(pltpu.make_async_copy(
                v_hbm.at[pl.ds(at, quarter), pl.ds(h * DV, DV)], vin.at[h, pl.ds(8 + at, quarter)],
                in_sem.at[n, 1 + h]))
        return copies

    for n in range(QUARTERS):
        for load in lin_loads(n):
            load.start()

    barrier = pltpu.get_barrier_semaphore()
    for step in range(1, seqs):
        pl.semaphore_signal(barrier, inc=1, device_id={"seq": lax.rem(me + step, seqs)}, device_id_type=MESH)
    for step in range(1, heads):
        pl.semaphore_signal(barrier, inc=1, device_id={"head": lax.rem(my_head + step, heads)}, device_id_type=MESH)

    def head_loads(h):
        columns = pl.ds(pl.multiple_of(h * DV, DV), DV)
        copies = [pltpu.make_async_copy(swa_hbm.at[0, :, columns], qin.at[h], swa_sem.at[h, 0])]
        for which in range(2):
            copies.append(pltpu.make_async_copy(
                swa_hbm.at[1 + which, :, columns], kin.at[which, h, pl.ds(WIN, tokens)], swa_sem.at[h, 1 + which]))
        return copies

    for h in range(local):
        for load in head_loads(h):
            load.start()
    after = {"seq": lax.rem(me + 1, seqs)}

    def remote(source, target, send, receive, device):
        return pltpu.make_async_remote_copy(
            src_ref=source, dst_ref=target, send_sem=send, recv_sem=receive, device_id=device, device_id_type=MESH)

    tail = pl.ds(tokens - 8, 8)
    halos = [remote(qk_hbm.at[tail], xin.at[pl.ds(0, 8)], hs_sem.at[0], hr_sem.at[0], after)]
    for h in range(local):
        halos.append(remote(v_hbm.at[tail, pl.ds(h * DV, DV)], vin.at[h, pl.ds(0, 8)],
                            hs_sem.at[1 + h], hr_sem.at[1 + h], after))
    window_halos = []
    for h in range(local):
        for which in range(2):
            slot = 1 + local + 2 * h + which
            window_halos.append(remote(
                swa_hbm.at[1 + which, pl.ds(tokens - WIN, WIN), pl.ds(h * DV, DV)],
                kin.at[which, h, pl.ds(0, WIN)], hs_sem.at[slot], hr_sem.at[slot], after))

    pl.semaphore_wait(barrier, seqs - 1 + heads - 1)
    for copy in halos + window_halos[::2]:
        copy.start()
    sx[0] = jnp.zeros(sx.shape[1:], F32)
    for load in lin_loads(0):
        load.wait()
    per_quarter = chunks // QUARTERS
    steps = chunks // 2

    def state_step(i, carry):
        last = i == steps - 1

        @pl.when((lax.rem(2 * i + 2, per_quarter) == 0) & jnp.logical_not(last))
        def _():
            for load in lin_loads((2 * i + 2) // per_quarter):
                load.wait()

        @pl.when(last)
        def _():
            for copy in halos:
                copy.wait_recv()
            keep = me > 0
            xin[pl.ds(0, 8)] = jnp.where(keep, xin[pl.ds(0, 8)], 0.0)
            for h in range(local):
                vin[h, pl.ds(0, 8)] = jnp.where(keep, vin[h, pl.ds(0, 8)], 0.0)

        which_chunks = (2 * i + 1, lax.rem(2 * i + 2, chunks))
        pairs = [(c, h) for c in range(2) for h in range(local)]
        turned = []
        for c in which_chunks:
            row = pl.multiple_of(c * C, C)
            x = wqk_ref[0:1] * xin[pl.ds(row + 6, C)]
            x = x + wqk_ref[1:2] * xin[pl.ds(row + 7, C)]
            x = x + wqk_ref[2:3] * xin[pl.ds(row + 8, C)]
            xs[pl.ds(row, C)] = x
            turned.append(x.T)
        boths = []
        for n, h in pairs:
            row = pl.multiple_of(which_chunks[n] * C, C)
            columns = slice(h * DV, (h + 1) * DV)
            u = wv_ref[0:1, columns] * vin[h, pl.ds(row + 6, C)]
            u = u + wv_ref[1:2, columns] * vin[h, pl.ds(row + 7, C)]
            u = u + wv_ref[2:3, columns] * vin[h, pl.ds(row + 8, C)]
            both = jnp.concatenate(split(u), axis=1)
            us[h, pl.ds(row, C)] = both
            boths.append(both)
        for c, value in zip(which_chunks, turned):
            for piece in range(2 * local):
                at = value[piece * DK:(piece + 1) * DK]
                xt[c, piece, 0:DK] = at
                xt[c, piece, DK:2 * DK] = at
        phis = []
        for n, h in pairs:
            c = which_chunks[n]
            phi = feature_rows(lambda start, size: xt[c, 2 * h + 1, start:start + size], 1, 1, 1.0)
            phis.append(jnp.concatenate(split(phi), axis=1))
        states = [dot(phi, jnp.concatenate([both, both], axis=0)) for phi, both in zip(phis, boths)]
        again = jnp.where(last, 0.0, 1.0).astype(F32)
        for h in range(local):
            rows = slice(h * ROWS, (h + 1) * ROWS)
            total = sx[2 * i, rows] + fold(states[h])
            sx[2 * i + 1, rows] = total
            sx[2 * i + 2, rows] = total * again + fold(states[local + h])
        return carry

    lax.fori_loop(0, steps, state_step, 0)

    mine[...] = sx[chunks - 1] + sx[chunks]
    first = []
    for step in far_first(seqs):
        peer = lax.rem(me + step, seqs)
        rows = pl.ds(pl.multiple_of(peer * part, 8), part)
        first.append(remote(mine.at[rows], got.at[me], s1.at[step - 1], r1.at[step - 1], {"seq": peer}))
        first[-1].start()
    got[me] = mine[pl.ds(pl.multiple_of(me * part, 8), part)]

    lane = lax.broadcasted_iota(jnp.int32, (C, C), 1)
    sub = lax.broadcasted_iota(jnp.int32, (C, C), 0)
    query_lane = lax.rem(lane, 2 * DK) < DK
    causal = lane <= sub

    def local_step(i, carry):
        which_chunks = [LOCAL_GROUP * i + n for n in range(LOCAL_GROUP)]
        at_rows = [pl.ds(pl.multiple_of(c * C, C), C) for c in which_chunks]
        lefts = []
        for rows in at_rows:
            x = xs[rows]
            lefts.append(jnp.concatenate(split(jnp.where(query_lane, x, pltpu.roll(x, DK, 1))), axis=1))
        rights = []
        for c in which_chunks:
            for pair in range(local // 2):
                sides = []
                for h in (2 * pair, 2 * pair + 1):
                    high, low = split(xt[c, 2 * h + 1, 0:DK])
                    blank = jnp.zeros((DK, C), BF16)
                    pieces = [blank] * (2 * 2 * local)
                    pieces[2 * h] = high
                    pieces[2 * h + 1] = low
                    pieces[2 * local + 2 * h] = high
                    sides.append(jnp.concatenate(pieces, axis=0))
                rights.append(jnp.concatenate(sides, axis=1))
        scores = [dot(lefts[n], rights[n * (local // 2) + pair])
                  for n in range(LOCAL_GROUP) for pair in range(local // 2)]
        values = []
        for score in scores:
            for which in range(2):
                value = score[:, which * C:(which + 1) * C] + 4.0
                value = jnp.where(causal, value * value + 16.0, 0.0)
                values.append(jnp.concatenate(split(value), axis=1))
        sums = []
        for n in range(LOCAL_GROUP):
            for h in range(local):
                both = us[h, at_rows[n]]
                sums.append(dot(values[n * local + h], jnp.concatenate([both, both], axis=0)))
        for n in range(LOCAL_GROUP):
            for h in range(local):
                lin[h, at_rows[n]] = fold(sums[n * local + h])
        return carry

    lax.fori_loop(0, chunks // LOCAL_GROUP, local_step, 0)

    own_rows = pl.ds(pl.multiple_of(me * part, 8), part)
    second = []
    for step in far_first(seqs):
        peer = lax.rem(me + step, seqs)
        second.append(remote(prefs.at[peer], pref.at[own_rows], s2.at[step - 1], r2.at[step - 1], {"seq": peer}))

    def prefix_step(d, carry):
        prefs[d] = carry
        return carry + got[d]

    key = lax.broadcasted_iota(jnp.int32, (WIN, C), 1)
    query = lax.broadcasted_iota(jnp.int32, (WIN, C), 0)
    scale = math.log2(math.e) / math.sqrt(DV)
    own_half = lax.rem(lax.broadcasted_iota(jnp.int32, (C, 2 * C), 1), C) < WIN
    inside = ((key < WIN) & (key <= query)) | ((key >= WIN) & (key - C > query - WIN))
    lowest = jnp.where(me == 0, C, 0)
    starts = inside & ((key < WIN) | (key >= lowest))
    bias_first = jnp.where(starts, 0.0, -1e30).astype(F32)
    bias_even = jnp.where(inside, 0.0, -1e30).astype(F32)
    bias_odd = jnp.where((key <= query + WIN) & (key > query), 0.0, -1e30).astype(F32)

    def split_queries(value):
        return jnp.concatenate(split(value * scale), axis=1)

    def split_values(h, j):
        return jnp.concatenate(split(kin[1, h, pl.ds(j * WIN, WIN)]), axis=1)

    def softmax(score):
        weight = jnp.exp2(score - jnp.max(score, axis=1, keepdims=True))
        return jnp.concatenate(split(weight), axis=1), jnp.sum(weight, axis=1, keepdims=True)

    def window_step(h, carry):
        @pl.when(h == PREFIX_HEAD)
        def _():
            for copy in first:
                copy.wait_recv()
            lax.fori_loop(0, seqs, prefix_step, jnp.zeros((part, DV), F32))
            for copy in second:
                copy.start()
            pref[own_rows] = prefs[me]
            for copy in window_halos[1::2]:
                copy.start()

        for load in head_loads(h):
            load.wait()
        tiles = [jnp.concatenate(split(kin[0, h, pl.ds(WIN + j * C, C)].T), axis=1) for j in range(chunks)]
        scores = []
        for j in range(chunks):
            own = tiles[j]
            q_both = split_queries(qin[h, pl.ds(j * C, C)])
            if j > 0:
                ring = jnp.where(own_half, own, tiles[j - 1])
                scores.append(fold(dot(q_both[:WIN], jnp.concatenate([ring, ring], axis=0))) + bias_even)
            scores.append(fold(dot(q_both[WIN:], jnp.concatenate([own, own], axis=0))) + bias_odd)
        weights = [softmax(score) for score in scores]
        values = [split_values(h, j) for j in range(1, 2 * chunks + 1)]
        for j, (weight, norm) in enumerate(weights, 1):
            even = j if j % 2 else j + 1
            odd = j + 1 if j % 2 else j
            tile = [values[even - 1], values[odd - 1]]
            win[h, pl.ds(j * WIN, WIN)] = fold(dot(weight, jnp.concatenate(tile + tile, axis=0))) / norm
        return carry

    lax.fori_loop(0, local, window_step, 0)

    def opening_step():
        for copy in window_halos:
            copy.wait_recv()
        rings = [jnp.concatenate(split(jnp.concatenate(
            [kin[0, h, pl.ds(WIN, WIN)], kin[0, h, pl.ds(0, WIN)]], axis=0).T), axis=1) for h in range(local)]
        openings = [fold(dot(split_queries(qin[h, pl.ds(0, WIN)]), jnp.concatenate([ring, ring], axis=0))) + bias_first
                    for h, ring in enumerate(rings)]
        for h, (weight, norm) in enumerate([softmax(score) for score in openings]):
            tile = [split_values(h, 1), split_values(h, 0)]
            win[h, pl.ds(0, WIN)] = fold(dot(weight, jnp.concatenate(tile + tile, axis=0))) / norm

    for copy in second:
        copy.wait_recv()

    def carried_step(i, carry):
        group = chunks // CARRIED_GROUP - 1 - i
        which_chunks = [CARRIED_GROUP * group + n for n in range(CARRIED_GROUP)]

        @pl.when(group == 0)
        def _():
            opening_step()

        at_rows = [pl.ds(pl.multiple_of(c * C, C), C) for c in which_chunks]
        pairs = [(n, h) for n in range(CARRIED_GROUP) for h in range(local)]
        phis = []
        for n, h in pairs:
            phi = feature_rows(
                lambda start, size: xt[which_chunks[n], 2 * h, start:start + size], 2.0, 8.0, 32.0)
            phis.append(jnp.concatenate(split(phi), axis=0).T)
        states = []
        for n, h in pairs:
            c = which_chunks[n]
            rows = slice(h * ROWS, (h + 1) * ROWS)
            later = jnp.where(c > 0, 1.0, 0.0).astype(F32)
            state = sx[jnp.maximum(c - 1, 0), rows] + (pref[rows] + sx[chunks, rows] * later)
            both = jnp.concatenate(split(state), axis=1)
            states.append(jnp.concatenate([both, both], axis=0))
        earlier = [dot(phi, state) for phi, state in zip(phis, states)]
        mixes = [lin[h, at_rows[n]] + fold(earlier[n * local + h]) for n, h in pairs]
        means = [jnp.sum(mix * mix, axis=1, keepdims=True) * (1.0 / DV) for mix in mixes]
        squares = [jnp.zeros((C, DV), F32) for _ in which_chunks]
        for (n, h), mix, mean in zip(pairs, mixes, means):
            columns = slice(h * DV, (h + 1) * DV)
            value = mix * lax.rsqrt(mean + 1024.0e-6) * gain_ref[0:1, columns] + win[h, at_rows[n]]
            out_ref[at_rows[n], columns] = value
            squares[n] = squares[n] + value * value
        for c, square in zip(which_chunks, squares):
            sq[c] = jnp.sum(square.T, axis=0, keepdims=True)
        return carry

    lax.fori_loop(0, chunks // CARRIED_GROUP, carried_step, 0)

    third = []
    for step in range(1, heads):
        peer = lax.rem(my_head + step, heads)
        third.append(remote(sq, sqgot.at[step - 1], s3.at[step - 1], r3.at[step - 1], {"head": peer}))
        third[-1].start()
    for copy in halos + window_halos + first + second:
        copy.wait_send()
    total = sq[...]
    for step, copy in enumerate(third):
        copy.wait_recv()
        total = total + sqgot[step]
    total_ref[...] = total
    for copy in third:
        copy.wait_send()


def scale_kernel(count, value_ref, total_ref, out_hbm, stage, sems):
    chunks, width = total_ref.shape[0], value_ref.shape[1]
    copies = []
    for c in range(chunks):
        rows = pl.ds(c * C, C)
        factor = lax.rsqrt(total_ref[c] * (1.0 / count) + 1e-06)
        factor = jnp.broadcast_to(factor, (C, C)).T
        for h in range(width // DV):
            columns = slice(h * DV, (h + 1) * DV)
            stage[rows, columns] = value_ref[rows, columns] * factor
        copies.append(pltpu.make_async_copy(stage.at[rows], out_hbm.at[rows], sems.at[c]))
        copies[-1].start()
    for copy in copies:
        copy.wait()


def per_device(seqs, heads, lin_qk, lin_v, conv_qk, conv_v, swa_qkv, head_gain):
    tokens = lin_qk.shape[0]
    width = lin_v.shape[1]
    local = width // DV
    chunks = tokens // C
    part = local * ROWS // seqs
    hbm = pl.BlockSpec(memory_space=pltpu.HBM)
    vmem = pl.BlockSpec(memory_space=pltpu.VMEM)
    dma = pltpu.SemaphoreType.DMA
    halos = 1 + 3 * local
    combined, squares = pl.pallas_call(
        functools.partial(kernel, seqs, heads),
        out_shape=(
            pltpu.VMEM((tokens, width), F32),
            pltpu.VMEM((chunks, 1, C), F32),
        ),
        in_specs=[hbm, hbm, hbm, vmem, vmem, vmem],
        out_specs=(vmem, vmem),
        scratch_shapes=[
            pltpu.VMEM((8 + tokens, 2 * DK * local), F32),
            pltpu.VMEM((local, 8 + tokens, DV), F32),
            pltpu.VMEM((local, tokens, DV), F32),
            pltpu.VMEM((2, local, WIN + tokens, DV), F32),
            pltpu.VMEM((tokens, 2 * DK * local), F32),
            pltpu.VMEM((chunks, 2 * local, 2 * DK, C), F32),
            pltpu.VMEM((local, tokens, 2 * DV), BF16),
            pltpu.VMEM((chunks + 1, local * ROWS, DV), F32),
            pltpu.VMEM((local, tokens, DV), F32),
            pltpu.VMEM((local, tokens, DV), F32),
            pltpu.VMEM((local * ROWS, DV), F32),
            pltpu.VMEM((seqs, part, DV), F32),
            pltpu.VMEM((seqs, part, DV), F32),
            pltpu.VMEM((local * ROWS, DV), F32),
            pltpu.VMEM((chunks, 1, C), F32),
            pltpu.VMEM((heads - 1, chunks, 1, C), F32),
            dma((QUARTERS, 1 + local)),
            dma((local, 3)),
            dma((halos,)),
            dma((halos,)),
            dma((seqs - 1,)),
            dma((seqs - 1,)),
            dma((seqs - 1,)),
            dma((seqs - 1,)),
            dma((heads - 1,)),
            dma((heads - 1,)),
        ],
        compiler_params=pltpu.CompilerParams(
            collective_id=0, has_side_effects=True, vmem_limit_bytes=54 * 1024 * 1024
        ),
        name="mixer",
    )(lin_qk, lin_v, jnp.transpose(swa_qkv, (1, 0, 2)), conv_qk, conv_v, head_gain[None])
    return pl.pallas_call(
        functools.partial(scale_kernel, heads * width),
        out_shape=jax.ShapeDtypeStruct((tokens, width), F32),
        in_specs=[vmem, vmem],
        out_specs=hbm,
        scratch_shapes=[pltpu.VMEM((tokens, width), F32), dma((chunks,))],
        compiler_params=pltpu.CompilerParams(vmem_limit_bytes=16 * 1024 * 1024),
        name="scale",
    )(combined, squares)


def solution(mesh):
    placed = (
        P("seq", "head"),
        P("seq", "head"),
        P(None, "head"),
        P(None, "head"),
        P("seq", None, "head"),
        P("head"),
    )
    return jax.shard_map(
        functools.partial(per_device, mesh.shape["seq"], mesh.shape["head"]),
        mesh=mesh, in_specs=placed, out_specs=P("seq", "head"), check_vma=False,
    )
```

```python
import functools
import math

import jax
import jax.numpy as jnp
from jax import lax
from jax.experimental import pallas as pl
from jax.experimental.pallas import tpu as pltpu
from jax.sharding import PartitionSpec as P

DK = 16
DV = 128
WIN = 64
C = 128
QUARTERS = 4
LOCAL_GROUP = 4
CARRIED_GROUP = 4
PREFIX_HEAD = 1
ROWS = 160
MESH = pl.DeviceIdType.MESH
F32 = jnp.float32
BF16 = jnp.bfloat16


def split(value):
    high = value.astype(BF16)
    low = (value - high.astype(F32)).astype(BF16)
    return high, low


def dot(left, right, dims=((1,), (0,))):
    return lax.dot_general(left, right, (dims, ((), ())), preferred_element_type=F32)


def fold(value):
    return value[:, :DV] + value[:, DV:]


def feature_rows(load, pair, linear, constant):
    base = load(0, DK)
    twice = base if pair == 1 else base * pair
    rows = [base * base]
    rows += [twice * load(shift, DK) for shift in range(1, DK // 2)]
    rows += [twice[: DK // 2] * load(DK // 2, DK // 2)]
    rows += [base if linear == 1 else base * linear]
    first = lax.broadcasted_iota(jnp.int32, (8, base.shape[1]), 0) == 0
    rows += [jnp.where(first, F32(constant), F32(0.0))]
    return jnp.concatenate(rows, axis=0)


def far_first(seqs):
    side = math.isqrt(seqs)
    return sorted(range(1, seqs), key=lambda step: -sum(
        min(at, side - at) for at in (step // side, step % side)))


def kernel(
    seqs, heads,
    qk_hbm, v_hbm, swa_hbm, wqk_ref, wv_ref, gain_ref,
    out_ref, total_ref,
    xin, vin, qin, kin, xs, xt, us, sx, lin, win,
    mine, got, prefs, pref, sq, sqgot,
    in_sem, swa_sem, hs_sem, hr_sem, s1, r1, s2, r2, s3, r3,
):
    tokens = xs.shape[0]
    local = vin.shape[0]
    chunks = tokens // C
    part = local * ROWS // seqs
    quarter = tokens // QUARTERS
    me = lax.axis_index("seq")
    my_head = lax.axis_index("head")

    def lin_loads(n):
        at = pl.multiple_of(n * quarter, 8)
        copies = [pltpu.make_async_copy(
            qk_hbm.at[pl.ds(at, quarter)], xin.at[pl.ds(8 + at, quarter)], in_sem.at[n, 0])]
        for h in range(local):
            copies.append(pltpu.make_async_copy(
                v_hbm.at[pl.ds(at, quarter), pl.ds(h * DV, DV)], vin.at[h, pl.ds(8 + at, quarter)],
                in_sem.at[n, 1 + h]))
        return copies

    for n in range(QUARTERS):
        for load in lin_loads(n):
            load.start()

    barrier = pltpu.get_barrier_semaphore()
    for step in range(1, seqs):
        pl.semaphore_signal(barrier, inc=1, device_id={"seq": lax.rem(me + step, seqs)}, device_id_type=MESH)
    for step in range(1, heads):
        pl.semaphore_signal(barrier, inc=1, device_id={"head": lax.rem(my_head + step, heads)}, device_id_type=MESH)

    def head_loads(h):
        columns = pl.ds(pl.multiple_of(h * DV, DV), DV)
        copies = [pltpu.make_async_copy(swa_hbm.at[0, :, columns], qin.at[h], swa_sem.at[h, 0])]
        for which in range(2):
            copies.append(pltpu.make_async_copy(
                swa_hbm.at[1 + which, :, columns], kin.at[which, h, pl.ds(WIN, tokens)], swa_sem.at[h, 1 + which]))
        return copies

    for h in range(local):
        for load in head_loads(h):
            load.start()
    after = {"seq": lax.rem(me + 1, seqs)}

    def remote(source, target, send, receive, device):
        return pltpu.make_async_remote_copy(
            src_ref=source, dst_ref=target, send_sem=send, recv_sem=receive, device_id=device, device_id_type=MESH)

    tail = pl.ds(tokens - 8, 8)
    halos = [remote(qk_hbm.at[tail], xin.at[pl.ds(0, 8)], hs_sem.at[0], hr_sem.at[0], after)]
    for h in range(local):
        halos.append(remote(v_hbm.at[tail, pl.ds(h * DV, DV)], vin.at[h, pl.ds(0, 8)],
                            hs_sem.at[1 + h], hr_sem.at[1 + h], after))
    window_halos = []
    for h in range(local):
        for which in range(2):
            slot = 1 + local + 2 * h + which
            window_halos.append(remote(
                swa_hbm.at[1 + which, pl.ds(tokens - WIN, WIN), pl.ds(h * DV, DV)],
                kin.at[which, h, pl.ds(0, WIN)], hs_sem.at[slot], hr_sem.at[slot], after))

    pl.semaphore_wait(barrier, seqs - 1 + heads - 1)
    for copy in halos + window_halos[::2]:
        copy.start()
    sx[0] = jnp.zeros(sx.shape[1:], F32)
    for load in lin_loads(0):
        load.wait()
    per_quarter = chunks // QUARTERS
    steps = chunks // 2

    def state_step(i, carry):
        last = i == steps - 1

        @pl.when((lax.rem(2 * i + 2, per_quarter) == 0) & jnp.logical_not(last))
        def _():
            for load in lin_loads((2 * i + 2) // per_quarter):
                load.wait()

        @pl.when(last)
        def _():
            for copy in halos:
                copy.wait_recv()
            keep = me > 0
            xin[pl.ds(0, 8)] = jnp.where(keep, xin[pl.ds(0, 8)], 0.0)
            for h in range(local):
                vin[h, pl.ds(0, 8)] = jnp.where(keep, vin[h, pl.ds(0, 8)], 0.0)

        which_chunks = (2 * i + 1, lax.rem(2 * i + 2, chunks))
        pairs = [(c, h) for c in range(2) for h in range(local)]
        turned = []
        for c in which_chunks:
            row = pl.multiple_of(c * C, C)
            x = wqk_ref[0:1] * xin[pl.ds(row + 6, C)]
            x = x + wqk_ref[1:2] * xin[pl.ds(row + 7, C)]
            x = x + wqk_ref[2:3] * xin[pl.ds(row + 8, C)]
            xs[pl.ds(row, C)] = x
            turned.append(x.T)
        boths = []
        for n, h in pairs:
            row = pl.multiple_of(which_chunks[n] * C, C)
            columns = slice(h * DV, (h + 1) * DV)
            u = wv_ref[0:1, columns] * vin[h, pl.ds(row + 6, C)]
            u = u + wv_ref[1:2, columns] * vin[h, pl.ds(row + 7, C)]
            u = u + wv_ref[2:3, columns] * vin[h, pl.ds(row + 8, C)]
            both = jnp.concatenate(split(u), axis=1)
            us[h, pl.ds(row, C)] = both
            boths.append(both)
        for c, value in zip(which_chunks, turned):
            for piece in range(2 * local):
                at = value[piece * DK:(piece + 1) * DK]
                xt[c, piece, 0:DK] = at
                xt[c, piece, DK:2 * DK] = at
        phis = []
        for n, h in pairs:
            c = which_chunks[n]
            phi = feature_rows(lambda start, size: xt[c, 2 * h + 1, start:start + size], 1, 1, 1.0)
            phis.append(jnp.concatenate(split(phi), axis=1))
        states = [dot(phi, jnp.concatenate([both, both], axis=0)) for phi, both in zip(phis, boths)]
        again = jnp.where(last, 0.0, 1.0).astype(F32)
        for h in range(local):
            rows = slice(h * ROWS, (h + 1) * ROWS)
            total = sx[2 * i, rows] + fold(states[h])
            sx[2 * i + 1, rows] = total
            sx[2 * i + 2, rows] = total * again + fold(states[local + h])
        return carry

    lax.fori_loop(0, steps, state_step, 0)

    mine[...] = sx[chunks - 1] + sx[chunks]
    first = []
    for step in far_first(seqs):
        peer = lax.rem(me + step, seqs)
        rows = pl.ds(pl.multiple_of(peer * part, 8), part)
        first.append(remote(mine.at[rows], got.at[me], s1.at[step - 1], r1.at[step - 1], {"seq": peer}))
        first[-1].start()
    got[me] = mine[pl.ds(pl.multiple_of(me * part, 8), part)]

    lane = lax.broadcasted_iota(jnp.int32, (C, C), 1)
    sub = lax.broadcasted_iota(jnp.int32, (C, C), 0)
    query_lane = lax.rem(lane, 2 * DK) < DK
    causal = lane <= sub

    def local_step(i, carry):
        which_chunks = [LOCAL_GROUP * i + n for n in range(LOCAL_GROUP)]
        at_rows = [pl.ds(pl.multiple_of(c * C, C), C) for c in which_chunks]
        lefts = []
        for rows in at_rows:
            x = xs[rows]
            lefts.append(jnp.concatenate(split(jnp.where(query_lane, x, pltpu.roll(x, DK, 1))), axis=1))
        rights = []
        for c in which_chunks:
            for pair in range(local // 2):
                sides = []
                for h in (2 * pair, 2 * pair + 1):
                    high, low = split(xt[c, 2 * h + 1, 0:DK])
                    blank = jnp.zeros((DK, C), BF16)
                    pieces = [blank] * (2 * 2 * local)
                    pieces[2 * h] = high
                    pieces[2 * h + 1] = low
                    pieces[2 * local + 2 * h] = high
                    sides.append(jnp.concatenate(pieces, axis=0))
                rights.append(jnp.concatenate(sides, axis=1))
        scores = [dot(lefts[n], rights[n * (local // 2) + pair])
                  for n in range(LOCAL_GROUP) for pair in range(local // 2)]
        values = []
        for score in scores:
            for which in range(2):
                value = score[:, which * C:(which + 1) * C] + 4.0
                value = jnp.where(causal, value * value + 16.0, 0.0)
                values.append(jnp.concatenate(split(value), axis=1))
        sums = []
        for n in range(LOCAL_GROUP):
            for h in range(local):
                both = us[h, at_rows[n]]
                sums.append(dot(values[n * local + h], jnp.concatenate([both, both], axis=0)))
        for n in range(LOCAL_GROUP):
            for h in range(local):
                lin[h, at_rows[n]] = fold(sums[n * local + h])
        return carry

    lax.fori_loop(0, chunks // LOCAL_GROUP, local_step, 0)

    own_rows = pl.ds(pl.multiple_of(me * part, 8), part)
    second = []
    for step in far_first(seqs):
        peer = lax.rem(me + step, seqs)
        second.append(remote(prefs.at[peer], pref.at[own_rows], s2.at[step - 1], r2.at[step - 1], {"seq": peer}))

    def prefix_step(d, carry):
        prefs[d] = carry
        return carry + got[d]

    key = lax.broadcasted_iota(jnp.int32, (WIN, C), 1)
    query = lax.broadcasted_iota(jnp.int32, (WIN, C), 0)
    scale = math.log2(math.e) / math.sqrt(DV)
    own_half = lax.rem(lax.broadcasted_iota(jnp.int32, (C, 2 * C), 1), C) < WIN
    inside = ((key < WIN) & (key <= query)) | ((key >= WIN) & (key - C > query - WIN))
    lowest = jnp.where(me == 0, C, 0)
    starts = inside & ((key < WIN) | (key >= lowest))
    bias_first = jnp.where(starts, 0.0, -1e30).astype(F32)
    bias_even = jnp.where(inside, 0.0, -1e30).astype(F32)
    bias_odd = jnp.where((key <= query + WIN) & (key > query), 0.0, -1e30).astype(F32)

    def split_queries(value):
        return jnp.concatenate(split(value * scale), axis=1)

    def split_values(h, j):
        return jnp.concatenate(split(kin[1, h, pl.ds(j * WIN, WIN)]), axis=1)

    def softmax(score):
        weight = jnp.exp2(score - jnp.max(score, axis=1, keepdims=True))
        return jnp.concatenate(split(weight), axis=1), jnp.sum(weight, axis=1, keepdims=True)

    def window_step(h, carry):
        @pl.when(h == PREFIX_HEAD)
        def _():
            for copy in first:
                copy.wait_recv()
            lax.fori_loop(0, seqs, prefix_step, jnp.zeros((part, DV), F32))
            for copy in second:
                copy.start()
            pref[own_rows] = prefs[me]
            for copy in window_halos[1::2]:
                copy.start()

        for load in head_loads(h):
            load.wait()
        tiles = [jnp.concatenate(split(kin[0, h, pl.ds(WIN + j * C, C)].T), axis=1) for j in range(chunks)]
        scores = []
        for j in range(chunks):
            own = tiles[j]
            q_both = split_queries(qin[h, pl.ds(j * C, C)])
            if j > 0:
                ring = jnp.where(own_half, own, tiles[j - 1])
                scores.append(fold(dot(q_both[:WIN], jnp.concatenate([ring, ring], axis=0))) + bias_even)
            scores.append(fold(dot(q_both[WIN:], jnp.concatenate([own, own], axis=0))) + bias_odd)
        weights = [softmax(score) for score in scores]
        values = [split_values(h, j) for j in range(1, 2 * chunks + 1)]
        for j, (weight, norm) in enumerate(weights, 1):
            even = j if j % 2 else j + 1
            odd = j + 1 if j % 2 else j
            tile = [values[even - 1], values[odd - 1]]
            win[h, pl.ds(j * WIN, WIN)] = fold(dot(weight, jnp.concatenate(tile + tile, axis=0))) / norm
        return carry

    lax.fori_loop(0, local, window_step, 0)

    def opening_step():
        for copy in window_halos:
            copy.wait_recv()
        rings = [jnp.concatenate(split(jnp.concatenate(
            [kin[0, h, pl.ds(WIN, WIN)], kin[0, h, pl.ds(0, WIN)]], axis=0).T), axis=1) for h in range(local)]
        openings = [fold(dot(split_queries(qin[h, pl.ds(0, WIN)]), jnp.concatenate([ring, ring], axis=0))) + bias_first
                    for h, ring in enumerate(rings)]
        for h, (weight, norm) in enumerate([softmax(score) for score in openings]):
            tile = [split_values(h, 1), split_values(h, 0)]
            win[h, pl.ds(0, WIN)] = fold(dot(weight, jnp.concatenate(tile + tile, axis=0))) / norm

    for copy in second:
        copy.wait_recv()

    def carried_step(i, carry):
        group = chunks // CARRIED_GROUP - 1 - i
        which_chunks = [CARRIED_GROUP * group + n for n in range(CARRIED_GROUP)]

        @pl.when(group == 0)
        def _():
            opening_step()

        at_rows = [pl.ds(pl.multiple_of(c * C, C), C) for c in which_chunks]
        pairs = [(n, h) for n in range(CARRIED_GROUP) for h in range(local)]
        phis = []
        for n, h in pairs:
            phi = feature_rows(
                lambda start, size: xt[which_chunks[n], 2 * h, start:start + size], 2.0, 8.0, 32.0)
            phis.append(jnp.concatenate(split(phi), axis=0).T)
        states = []
        for n, h in pairs:
            c = which_chunks[n]
            rows = slice(h * ROWS, (h + 1) * ROWS)
            later = jnp.where(c > 0, 1.0, 0.0).astype(F32)
            state = sx[jnp.maximum(c - 1, 0), rows] + (pref[rows] + sx[chunks, rows] * later)
            both = jnp.concatenate(split(state), axis=1)
            states.append(jnp.concatenate([both, both], axis=0))
        earlier = [dot(phi, state) for phi, state in zip(phis, states)]
        mixes = [lin[h, at_rows[n]] + fold(earlier[n * local + h]) for n, h in pairs]
        means = [jnp.sum(mix * mix, axis=1, keepdims=True) * (1.0 / DV) for mix in mixes]
        squares = [jnp.zeros((C, DV), F32) for _ in which_chunks]
        for (n, h), mix, mean in zip(pairs, mixes, means):
            columns = slice(h * DV, (h + 1) * DV)
            value = mix * lax.rsqrt(mean + 1024.0e-6) * gain_ref[0:1, columns] + win[h, at_rows[n]]
            out_ref[at_rows[n], columns] = value
            squares[n] = squares[n] + value * value
        for c, square in zip(which_chunks, squares):
            sq[c] = jnp.sum(square.T, axis=0, keepdims=True)
        return carry

    lax.fori_loop(0, chunks // CARRIED_GROUP, carried_step, 0)

    third = []
    for step in range(1, heads):
        peer = lax.rem(my_head + step, heads)
        third.append(remote(sq, sqgot.at[step - 1], s3.at[step - 1], r3.at[step - 1], {"head": peer}))
        third[-1].start()
    for copy in halos + window_halos + first + second:
        copy.wait_send()
    total = sq[...]
    for step, copy in enumerate(third):
        copy.wait_recv()
        total = total + sqgot[step]
    total_ref[...] = total
    for copy in third:
        copy.wait_send()


def scale_kernel(count, value_ref, total_ref, out_hbm, stage, sems):
    chunks, width = total_ref.shape[0], value_ref.shape[1]
    copies = []
    for c in range(chunks):
        rows = pl.ds(c * C, C)
        factor = lax.rsqrt(total_ref[c] * (1.0 / count) + 1e-06)
        factor = jnp.broadcast_to(factor, (C, C)).T
        for h in range(width // DV):
            columns = slice(h * DV, (h + 1) * DV)
            stage[rows, columns] = value_ref[rows, columns] * factor
        copies.append(pltpu.make_async_copy(stage.at[rows], out_hbm.at[rows], sems.at[c]))
        copies[-1].start()
    for copy in copies:
        copy.wait()


def per_device(seqs, heads, lin_qk, lin_v, conv_qk, conv_v, swa_qkv, head_gain):
    tokens = lin_qk.shape[0]
    width = lin_v.shape[1]
    local = width // DV
    chunks = tokens // C
    part = local * ROWS // seqs
    hbm = pl.BlockSpec(memory_space=pltpu.HBM)
    vmem = pl.BlockSpec(memory_space=pltpu.VMEM)
    dma = pltpu.SemaphoreType.DMA
    halos = 1 + 3 * local
    combined, squares = pl.pallas_call(
        functools.partial(kernel, seqs, heads),
        out_shape=(
            pltpu.VMEM((tokens, width), F32),
            pltpu.VMEM((chunks, 1, C), F32),
        ),
        in_specs=[hbm, hbm, hbm, vmem, vmem, vmem],
        out_specs=(vmem, vmem),
        scratch_shapes=[
            pltpu.VMEM((8 + tokens, 2 * DK * local), F32),
            pltpu.VMEM((local, 8 + tokens, DV), F32),
            pltpu.VMEM((local, tokens, DV), F32),
            pltpu.VMEM((2, local, WIN + tokens, DV), F32),
            pltpu.VMEM((tokens, 2 * DK * local), F32),
            pltpu.VMEM((chunks, 2 * local, 2 * DK, C), F32),
            pltpu.VMEM((local, tokens, 2 * DV), BF16),
            pltpu.VMEM((chunks + 1, local * ROWS, DV), F32),
            pltpu.VMEM((local, tokens, DV), F32),
            pltpu.VMEM((local, tokens, DV), F32),
            pltpu.VMEM((local * ROWS, DV), F32),
            pltpu.VMEM((seqs, part, DV), F32),
            pltpu.VMEM((seqs, part, DV), F32),
            pltpu.VMEM((local * ROWS, DV), F32),
            pltpu.VMEM((chunks, 1, C), F32),
            pltpu.VMEM((heads - 1, chunks, 1, C), F32),
            dma((QUARTERS, 1 + local)),
            dma((local, 3)),
            dma((halos,)),
            dma((halos,)),
            dma((seqs - 1,)),
            dma((seqs - 1,)),
            dma((seqs - 1,)),
            dma((seqs - 1,)),
            dma((heads - 1,)),
            dma((heads - 1,)),
        ],
        compiler_params=pltpu.CompilerParams(
            collective_id=0, has_side_effects=True, vmem_limit_bytes=54 * 1024 * 1024
        ),
        name="mixer",
    )(lin_qk, lin_v, jnp.transpose(swa_qkv, (1, 0, 2)), conv_qk, conv_v, head_gain[None])
    return pl.pallas_call(
        functools.partial(scale_kernel, heads * width),
        out_shape=jax.ShapeDtypeStruct((tokens, width), F32),
        in_specs=[vmem, vmem],
        out_specs=hbm,
        scratch_shapes=[pltpu.VMEM((tokens, width), F32), dma((chunks,))],
        compiler_params=pltpu.CompilerParams(vmem_limit_bytes=16 * 1024 * 1024),
        name="scale",
    )(combined, squares)


def solution(mesh):
    placed = (
        P("seq", "head"),
        P("seq", "head"),
        P(None, "head"),
        P(None, "head"),
        P("seq", None, "head"),
        P("head"),
    )
    return jax.shard_map(
        functools.partial(per_device, mesh.shape["seq"], mesh.shape["head"]),
        mesh=mesh, in_specs=placed, out_specs=P("seq", "head"), check_vma=False,
    )
```
